256 devices in a mesh: dp: 8 (over y, core), ctx: 32 (over z, x).
Axes of the slice: x: 4, y: 4, z: 8, core: 2. Of those that a mesh axis runs over, the one named last changes fastest.
Arguments:
- conv_input: bfloat16 [32768, 7424], P(('dp', 'ctx')), parts along dimension 0, may hold values from -6 to 6
- gate_input: bfloat16 [32768, 7168], P(('dp', 'ctx')), parts along dimension 0, may hold values from -6 to 6
- step_raw: float32 [32768, 112], P(('dp', 'ctx')), parts along dimension 0, may hold values from -2 to 24
- step_bias: float32 [112], replicated, may hold values from -13 to 0
- decay_log: float32 [112], replicated, may hold values from -3.3 to -1.6
- skip_weight: float32 [112], replicated, may hold values from 0.3 to 1.2
- conv_weight: float32 [4, 7424], replicated, may hold values from -3 to 3
- conv_bias: float32 [7424], replicated, may hold values from -3 to 3
- norm_gain: float32 [7168], replicated, may hold values from 0.25 to 1.75
- queries: bfloat16 [32768, 7168], P(('dp', 'ctx')), parts along dimension 0, may hold values from -130 to 130
- key_rows: bfloat16 [32768, 7168], P(('dp', 'ctx')), parts along dimension 0, may hold values from -10 to 10
Outputs:
- mamba_out: bfloat16 [32768, 7168], P(('dp', 'ctx')), parts along dimension 0
- attended: bfloat16 [32768, 7168], P(('dp', 'ctx')), parts along dimension 0
The draws below stay inside these ranges and needn't reach their ends.
There are 8 independent parts, one for each index of `dp`. The reference program is written for one: setup_inputs(seed, part) draws one part's arguments, and reference() takes and returns one part's arrays. A program takes and returns all parts, laid end to end along the dimension named above; an argument that names none is the same for every part. Nothing has to cross between parts.
All inputs are finite; a program needn't handle non-finite values.
Results may differ from the reference program's by a relative error of at most 0.005.
Values may be sent and summed in bfloat16 or wider, within the bound.
No kernel may reach another device: no remote copies, remote signals or barrier semaphores. Data moves between devices by JAX's collectives and lax.ppermute only.
A program may use at most 320 MiB of HBM per device.

```python
import math
import jax
import jax.numpy as jnp
from jax import lax

HEADS = 112
HEAD_DIM = 64
STATE = 64
GROUPS = 2
CONV = 4
ATT_HEADS = 32
ATT_DIM = 224
TOK_DEV = 128
SEQUENCE_TOKENS = 4096
INNER = 7168
CONV_CH = 7424


def head_kinds(key, share):
    return jax.random.randint(jax.random.fold_in(key, 90), (HEADS,), 0, 100) < share


def drawn_rows(key):
    base_rows = jax.random.normal(jax.random.fold_in(key, 71), (SEQUENCE_TOKENS, INNER), jnp.float32)
    base_rows = jnp.clip(base_rows, -6.0, 6.0)
    return base_rows


def draw_step_raw(key, part):
    key = jax.random.fold_in(key, 3)
    first, second, third, fourth = jax.random.split(key, 4)
    random_noise = jax.random.uniform(first, (SEQUENCE_TOKENS, HEADS), jnp.float32, -0.7, 0.7)
    block_offset_steps = jax.random.uniform(second, (SEQUENCE_TOKENS // TOK_DEV, 1, HEADS), jnp.float32, -0.7, 0.7)
    block_offset_steps = jnp.broadcast_to(block_offset_steps, (SEQUENCE_TOKENS // TOK_DEV, TOK_DEV, HEADS)).reshape(SEQUENCE_TOKENS, HEADS)
    chosen_places = jax.random.randint(third, (3,), 0, SEQUENCE_TOKENS)
    sudden_spike = jnp.any(jnp.arange(SEQUENCE_TOKENS)[:, None] == chosen_places[None, :], axis=1)
    level = jax.random.uniform(fourth, (SEQUENCE_TOKENS, HEADS), jnp.float32, 1.3, 2.5)
    raised_values = jnp.log(jnp.expm1(level)) - jnp.log(1.5 / SEQUENCE_TOKENS)
    return jnp.where(sudden_spike[:, None], raised_values, random_noise + block_offset_steps)


def draw_step_bias(key, part):
    share = 50
    slow_heads = head_kinds(key, share)
    key = jax.random.fold_in(key, 5)
    first, second = jax.random.split(key, 2)
    slow_bias = math.log(1.5 / SEQUENCE_TOKENS) + jax.random.uniform(first, (HEADS,), jnp.float32, -0.2, 0.2)
    fast_bias = jax.random.uniform(second, (HEADS,), jnp.float32, -1.5, 0.0)
    return jnp.where(slow_heads, slow_bias, fast_bias)


def draw_decay_log(key, part):
    share = 50
    slow_heads = head_kinds(key, share)
    key = jax.random.fold_in(key, 7)
    first, second = jax.random.split(key, 2)
    slow_rate = jnp.log(jax.random.uniform(first, (HEADS,), jnp.float32, 0.15, 0.2))
    fast_rate = jax.random.uniform(second, (HEADS,), jnp.float32, math.log(0.04), math.log(0.12))
    return jnp.where(slow_heads, slow_rate, fast_rate)


def draw_queries(key, part):
    key = jax.random.fold_in(key, 11)
    own_rows = jnp.clip(jax.random.normal(key, (SEQUENCE_TOKENS, INNER), jnp.float32), -6.0, 6.0)
    return own_rows.astype(jnp.bfloat16)


def draw_key_rows(key, part):
    base_rows = drawn_rows(key)
    result = base_rows
    return result.astype(jnp.bfloat16)


def steps_of(key, extent, cuts, smallest, top_value):
    def one(dim, blocks):
        draws = jax.random.uniform(jax.random.fold_in(jax.random.fold_in(key, 6), dim), (blocks,), jnp.float32, smallest / len(cuts), top_value / len(cuts))
        return jnp.repeat(jnp.exp(draws), extent[dim] // blocks).reshape((-1,) + (1,) * (len(extent) - dim - 1))

    factor_of = one(*cuts[0])
    for cut in cuts[1:]:
        factor_of = factor_of * one(*cut)
    return factor_of


def gaussian(own_key, dims, width, bound, cuts=(), kind=jnp.bfloat16):
    values = width * jax.random.normal(own_key, dims, jnp.float32)
    if cuts:
        values = values * steps_of(own_key, dims, cuts, -0.22, 0.18)
    return jnp.clip(values, -bound, bound).astype(kind)


def setup_inputs(seed: int = 0, part: int = 0) -> dict:
    keys = jax.random.split(jax.random.key(seed), 12)
    own_keys = jax.random.split(jax.random.fold_in(keys[11], part), 12)
    conv_input = gaussian(own_keys[0], (SEQUENCE_TOKENS, CONV_CH), 1.0, 6.0, ((0, 32),))
    gate_input = gaussian(own_keys[1], (SEQUENCE_TOKENS, INNER), 1.0, 6.0, ((0, 32),))
    step_raw = draw_step_raw(jax.random.fold_in(jax.random.fold_in(keys[11], part), 71), part)
    step_bias = draw_step_bias(jax.random.fold_in(keys[11], 71), part)
    decay_log = draw_decay_log(jax.random.fold_in(keys[11], 71), part)
    skip_weight = jnp.clip(jax.random.uniform(keys[5], (HEADS,), jnp.float32, 0.3, 1.2), 0.3, 1.2)
    conv_weight = gaussian(keys[6], (CONV, CONV_CH), CONV ** -0.5, 3.0, (), jnp.float32)
    conv_bias = gaussian(keys[7], (CONV_CH,), 0.5, 3.0, (), jnp.float32)
    norm_gain = jnp.clip(1.0 + 0.15 * jax.random.normal(keys[8], (INNER,), jnp.float32), 0.25, 1.75)
    queries = draw_queries(jax.random.fold_in(jax.random.fold_in(keys[11], part), 71), part)
    key_rows = draw_key_rows(jax.random.fold_in(jax.random.fold_in(keys[11], part), 71), part)
    return dict(conv_input=conv_input, gate_input=gate_input, step_raw=step_raw, step_bias=step_bias, decay_log=decay_log, skip_weight=skip_weight, conv_weight=conv_weight, conv_bias=conv_bias, norm_gain=norm_gain, queries=queries, key_rows=key_rows)


dt_cap = 3.0
eps = 1e-05

def convolve(padded, conv_weight, conv_bias, row_count):
    total = conv_bias[None, :] + conv_weight[0][None, :] * padded[0:row_count]
    for tap_index in range(1, conv_weight.shape[0]):
        total = total + conv_weight[tap_index][None, :] * padded[tap_index:tap_index + row_count]
    return jax.nn.silu(total).astype(jnp.bfloat16)

def span_terms(inputs, step_rates, decay_rate):
    row_count = inputs.shape[0]
    inner_width = HEADS * HEAD_DIM
    head_share = HEADS // GROUPS
    values = inputs[:, :inner_width].astype(jnp.float32).reshape(row_count, GROUPS, head_share, HEAD_DIM)
    writes_low = inputs[:, inner_width:inner_width + GROUPS * STATE].reshape(row_count, GROUPS, STATE)
    readout_low = inputs[:, inner_width + GROUPS * STATE:].reshape(row_count, GROUPS, STATE)
    writes = writes_low.astype(jnp.float32)
    readout = readout_low.astype(jnp.float32)
    grouped_rates = step_rates.reshape(row_count, GROUPS, head_share)
    running = jnp.cumsum(grouped_rates * decay_rate.reshape(GROUPS, head_share)[None], axis=0)
    running_heads = running.transpose(1, 2, 0)
    rates_heads = grouped_rates.transpose(1, 2, 0)
    positions = jnp.arange(row_count, dtype=jnp.int32)
    causal = (positions[:, None] >= positions[None, :])[None, None]
    spread = running_heads[:, :, :, None] - running_heads[:, :, None, :]
    fading = jnp.exp(jnp.where(causal, spread, -jnp.inf))
    intersection = jnp.einsum('tgn,sgn->gts', readout_low, writes_low, preferred_element_type=jnp.float32)
    mixing = intersection[:, None] * fading * rates_heads[:, :, None, :]
    inside = jnp.einsum('gkts,sgkp->tgkp', mixing, values, precision=lax.Precision.HIGHEST)
    trailing_decay = jnp.exp(running[-1])
    carry_weight = jnp.exp(running[-1][None] - running) * grouped_rates
    local_state = jnp.einsum('sgk,sgkp,sgn->gkpn', carry_weight, values, writes, precision=lax.Precision.HIGHEST)
    return (values, readout, running, inside, trailing_decay, local_state)

def carried(readout, running, state_in):
    across = jnp.einsum('tgn,gkpn->tgkp', readout, state_in, precision=lax.Precision.HIGHEST)
    return across * jnp.exp(running)[..., None]

def gated_norm(state_output, gate_input, norm_gain):
    row_count = state_output.shape[0]
    gate_values = gate_input.astype(jnp.float32).reshape(row_count, GROUPS, -1)
    gated_values = state_output.reshape(row_count, GROUPS, -1) * jax.nn.silu(gate_values)
    norm_scale = lax.rsqrt(lax.optimization_barrier(jnp.mean(gated_values * gated_values, axis=-1, keepdims=True)) + eps)
    normed = gated_values * norm_scale * norm_gain.reshape(GROUPS, -1)[None]
    return normed.reshape(row_count, -1).astype(jnp.bfloat16)

def reference(conv_input, gate_input, step_raw, step_bias, decay_log, skip_weight, conv_weight, conv_bias, norm_gain, queries, key_rows):
    padded = jnp.concatenate([jnp.zeros((CONV - 1, CONV_CH), jnp.float32), conv_input.astype(jnp.float32)], axis=0)
    inputs = convolve(padded, conv_weight, conv_bias, SEQUENCE_TOKENS)
    step_rates = jnp.minimum(jax.nn.softplus(step_raw + step_bias[None, :]), dt_cap)
    decay_rate = -jnp.exp(decay_log)
    skip_gain = skip_weight.reshape(GROUPS, HEADS // GROUPS)[None, :, :, None]
    blocks = SEQUENCE_TOKENS // TOK_DEV

    def advance(state_now, pieces):
        block_in, block_rates = pieces
        values, readout, running, inside, trailing_decay, local_state = span_terms(block_in, block_rates, decay_rate)
        state_output = inside + carried(readout, running, state_now) + skip_gain * values
        return (trailing_decay[:, :, None, None] * state_now + local_state, state_output)
    start_state = jnp.zeros((GROUPS, HEADS // GROUPS, HEAD_DIM, STATE), jnp.float32)
    final_state, state_output = lax.scan(advance, start_state, (inputs.reshape(blocks, TOK_DEV, CONV_CH), step_rates.reshape(blocks, TOK_DEV, HEADS)))
    mamba_out = gated_norm(state_output.reshape(SEQUENCE_TOKENS, GROUPS, HEADS // GROUPS, HEAD_DIM), gate_input, norm_gain)
    score_scale = 1.0 / math.sqrt(ATT_DIM)
    positions = jnp.arange(SEQUENCE_TOKENS, dtype=jnp.int32)
    causal = positions[:, None] >= positions[None, :]

    def per_head(head_index):
        offset = (head_index * ATT_DIM).astype(jnp.int32)
        query_slice = lax.dynamic_slice_in_dim(queries, offset, ATT_DIM, 1)
        key_part = lax.dynamic_slice_in_dim(key_rows, offset, ATT_DIM, 1)
        value_part = lax.dynamic_slice_in_dim(mamba_out, offset, ATT_DIM, 1)
        scores = jnp.dot(query_slice, key_part.T, preferred_element_type=jnp.float32) * score_scale
        scores = jnp.where(causal, scores, -jnp.inf)
        row_max = lax.optimization_barrier(jnp.max(scores, axis=1, keepdims=True))
        exponent = jnp.exp(scores - row_max)
        weights = (exponent / lax.optimization_barrier(jnp.sum(exponent, axis=1, keepdims=True))).astype(jnp.bfloat16)
        return jnp.dot(weights, value_part, preferred_element_type=jnp.float32).astype(jnp.bfloat16)
    head_outputs = lax.map(per_head, jnp.arange(ATT_HEADS, dtype=jnp.int32))
    attended = head_outputs.transpose(1, 0, 2).reshape(SEQUENCE_TOKENS, INNER)
    return (mamba_out, attended)
```

```python
import math

import jax
import jax.numpy as jnp
from jax import lax
from jax.experimental import pallas as pl
from jax.experimental.pallas import tpu as pltpu
from jax.sharding import PartitionSpec as P

HEADS = 112
HEAD_DIM = 64
STATE = 64
GROUPS = 2
CONV = 4
ATT_DIM = 224
INNER = HEADS * HEAD_DIM
ROW_PARTS = 4
COL_PARTS = 8
PART_ROWS = STATE // ROW_PARTS
PART_COLS = INNER // COL_PARTS

dt_cap = 3.0
eps = 1e-05
HIGHEST = lax.Precision.HIGHEST


def shifted(array, axis, by):
    size = lax.axis_size(axis)
    pairs = [(i, i + by) for i in range(size) if 0 <= i + by < size]
    return lax.ppermute(array, axis, pairs)


def convolve(padded, conv_weight, conv_bias, row_count):
    total = conv_bias[None, :] + conv_weight[0][None, :] * padded[0:row_count]
    for tap_index in range(1, conv_weight.shape[0]):
        total = total + conv_weight[tap_index][None, :] * padded[tap_index : tap_index + row_count]
    return jax.nn.silu(total).astype(jnp.bfloat16)


def scan_kernel(decay_ref, state_ref, out_ref):
    state = jnp.zeros(state_ref.shape[1:], jnp.float32)
    for block in range(state_ref.shape[0]):
        out_ref[block] = state.astype(out_ref.dtype)
        state = state * decay_ref[block] + state_ref[block].astype(jnp.float32)


def states_before(local_state, block_decay):
    size, index = lax.axis_size("ctx"), lax.axis_index("ctx")
    parts = local_state.astype(jnp.bfloat16).reshape(ROW_PARTS, PART_ROWS, COL_PARTS, PART_COLS)
    parts = parts.transpose(0, 2, 1, 3).reshape(size, PART_ROWS, PART_COLS)
    all_decay = lax.all_gather(block_decay, "ctx")
    heads = PART_COLS // HEAD_DIM
    own_decay = lax.dynamic_slice_in_dim(all_decay, (index % COL_PARTS) * heads, heads, 1)
    own_decay = jnp.repeat(own_decay, HEAD_DIM, axis=1)[:, None, :]
    blocks = lax.all_to_all(parts, "ctx", 0, 0, tiled=True)
    before = pl.pallas_call(
        scan_kernel,
        out_shape=jax.ShapeDtypeStruct(blocks.shape, jnp.bfloat16),
        compiler_params=pltpu.CompilerParams(vmem_limit_bytes=32 * 1024 * 1024),
    )(own_decay, blocks)
    state_in = lax.all_to_all(before, "ctx", 0, 0, tiled=True)
    state_in = state_in.reshape(ROW_PARTS, COL_PARTS, PART_ROWS, PART_COLS).transpose(0, 2, 1, 3)
    return state_in.reshape(STATE, INNER)


def gated_norm(state_output, gate_input, norm_gain):
    row_count = state_output.shape[0]
    gate_values = gate_input.astype(jnp.float32).reshape(row_count, GROUPS, -1)
    gated_values = state_output.reshape(row_count, GROUPS, -1) * jax.nn.silu(gate_values)
    norm_scale = lax.rsqrt(jnp.mean(gated_values * gated_values, axis=-1, keepdims=True) + eps)
    normed = gated_values * norm_scale * norm_gain.reshape(GROUPS, -1)[None]
    return normed.reshape(row_count, -1).astype(jnp.bfloat16)


def attend(head_queries, head_keys, head_values):
    total_rows = head_queries.shape[0]
    local_heads = head_queries.shape[1] // ATT_DIM
    query_all = head_queries.reshape(total_rows, local_heads, ATT_DIM)
    key_all = head_keys.reshape(total_rows, local_heads, ATT_DIM)
    value_all = head_values.reshape(total_rows, local_heads, ATT_DIM)
    score_scale = 1.0 / math.sqrt(ATT_DIM)
    block_rows = total_rows // 8
    pieces = []
    for block_index in range(8):
        block_stop = (block_index + 1) * block_rows
        query_block = query_all[block_index * block_rows : block_stop]
        scores = (
            jnp.einsum(
                "qhd,khd->hqk",
                query_block,
                key_all[:block_stop],
                preferred_element_type=jnp.float32,
            )
            * score_scale
        )
        query_pos = block_index * block_rows + jnp.arange(block_rows, dtype=jnp.int32)
        key_pos = jnp.arange(block_stop, dtype=jnp.int32)
        scores = jnp.where(key_pos[None, None, :] <= query_pos[None, :, None], scores, -jnp.inf)
        row_max = jnp.max(scores, axis=2, keepdims=True)
        exponent = jnp.exp(scores - row_max)
        weights = (exponent / jnp.sum(exponent, axis=2, keepdims=True)).astype(jnp.bfloat16)
        result = jnp.einsum(
            "hqk,khd->qhd", weights, value_all[:block_stop], preferred_element_type=jnp.float32
        )
        pieces.append(result.astype(jnp.bfloat16).reshape(block_rows, local_heads * ATT_DIM))
    return jnp.concatenate(pieces, axis=0)


def local(
    conv_input,
    gate_input,
    step_raw,
    step_bias,
    decay_log,
    skip_weight,
    conv_weight,
    conv_bias,
    norm_gain,
    queries,
    key_rows,
):
    row_count = conv_input.shape[0]
    share = HEADS // GROUPS
    before = shifted(conv_input[row_count - (CONV - 1) :], "ctx", 1)
    padded = jnp.concatenate([before.astype(jnp.float32), conv_input.astype(jnp.float32)], axis=0)
    inputs = convolve(padded, conv_weight, conv_bias, row_count)
    step_rates = jnp.minimum(jax.nn.softplus(step_raw + step_bias[None, :]), dt_cap)
    decay_rate = -jnp.exp(decay_log)
    running = jnp.cumsum(step_rates * decay_rate[None], axis=0)
    values = inputs[:, :INNER].astype(jnp.float32)
    writes = inputs[:, INNER : INNER + GROUPS * STATE].reshape(row_count, GROUPS, STATE)
    readout = inputs[:, INNER + GROUPS * STATE :].reshape(row_count, GROUPS, STATE)
    carry_weight = jnp.exp(running[-1][None] - running) * step_rates
    weighted = values * jnp.repeat(carry_weight, HEAD_DIM, axis=1)
    local_state = jnp.concatenate(
        [
            jnp.einsum(
                "sn,sc->nc",
                writes[:, g].astype(jnp.float32),
                weighted[:, g * share * HEAD_DIM : (g + 1) * share * HEAD_DIM],
                precision=HIGHEST,
            )
            for g in range(GROUPS)
        ],
        axis=1,
    )
    state_in = states_before(local_state, jnp.exp(running[-1]))

    running_heads = running.T.reshape(GROUPS, share, row_count)
    rates_heads = step_rates.T.reshape(GROUPS, share, row_count)
    positions = jnp.arange(row_count, dtype=jnp.int32)
    causal = (positions[:, None] >= positions[None, :])[None, None]
    spread = running_heads[:, :, :, None] - running_heads[:, :, None, :]
    fading = jnp.exp(jnp.where(causal, spread, -jnp.inf))
    intersection = jnp.einsum("tgn,sgn->gts", readout, writes, preferred_element_type=jnp.float32)
    mixing = intersection[:, None] * fading * rates_heads[:, :, None, :]
    grouped = values.reshape(row_count, GROUPS, share, HEAD_DIM)
    inside = jnp.einsum("gkts,sgkp->tgkp", mixing, grouped, precision=HIGHEST)
    state_output = inside.reshape(row_count, INNER) + jnp.repeat(skip_weight, HEAD_DIM)[None] * values

    across = jnp.concatenate(
        [
            jnp.einsum(
                "tn,nc->tc",
                readout[:, g],
                state_in[:, g * share * HEAD_DIM : (g + 1) * share * HEAD_DIM],
                preferred_element_type=jnp.float32,
            )
            for g in range(GROUPS)
        ],
        axis=1,
    )
    state_output = state_output + across * jnp.repeat(jnp.exp(running), HEAD_DIM, axis=1)
    mamba_out = gated_norm(state_output, gate_input, norm_gain)
    head_queries, head_keys, head_values = (
        lax.all_to_all(queries, "ctx", split_axis=1, concat_axis=0, tiled=True),
        lax.all_to_all(key_rows, "ctx", split_axis=1, concat_axis=0, tiled=True),
        lax.all_to_all(mamba_out, "ctx", split_axis=1, concat_axis=0, tiled=True),
    )
    attended_heads = attend(head_queries, head_keys, head_values)
    attended = lax.all_to_all(attended_heads, "ctx", split_axis=0, concat_axis=1, tiled=True)
    return (mamba_out, attended)


def solution(mesh):
    rows = P(("dp", "ctx"), None)
    placed = (rows, rows, rows, P(), P(), P(), P(), P(), P(), rows, rows)
    return jax.shard_map(
        local, mesh=mesh, in_specs=placed, out_specs=(rows, rows), check_vma=False
    )
```

```python
import functools
import math

import jax
import jax.numpy as jnp
from jax import lax
from jax.experimental import pallas as pl
from jax.experimental.pallas import tpu as pltpu
from jax.sharding import PartitionSpec as P

HEADS = 112
HEAD_DIM = 64
STATE = 64
GROUPS = 2
CONV = 4
ATT_DIM = 224
INNER = HEADS * HEAD_DIM
SHARE = INNER // GROUPS

ROW_PARTS = 4
COL_PARTS = 8
PART_ROWS = STATE // ROW_PARTS
PART_COLS = INNER // COL_PARTS
LANES = 128
PART_TILES = PART_COLS // LANES
PART_HEADS = PART_COLS // HEAD_DIM
STATE_ROWS = PART_TILES * PART_ROWS

QUERY_BLOCK = 512
KEY_BLOCK = 1024

dt_cap = 3.0
eps = 1e-05
HIGHEST = lax.Precision.HIGHEST
VMEM_LIMIT = 56 * 1024 * 1024
PARAMS = pltpu.CompilerParams(vmem_limit_bytes=VMEM_LIMIT)


def shifted(array, axis, by):
    size = lax.axis_size(axis)
    pairs = [(i, i + by) for i in range(size) if 0 <= i + by < size]
    return lax.ppermute(array, axis, pairs)


def exchanged(array):
    return lax.all_to_all(array, "ctx", 0, 0, tiled=True)


def convolve(padded, conv_weight, conv_bias, row_count):
    total = conv_bias[None, :] + conv_weight[0][None, :] * padded[0:row_count]
    for tap_index in range(1, conv_weight.shape[0]):
        total = total + conv_weight[tap_index][None, :] * padded[tap_index : tap_index + row_count]
    return jax.nn.silu(total).astype(jnp.bfloat16)


def per_channel(by_head):
    return jnp.repeat(by_head, HEAD_DIM, axis=-1)


def turn_kernel(query_ref, key_ref, out_ref):
    heads = out_ref.shape[0]
    for source, offset in ((query_ref, 0), (key_ref, ATT_DIM)):
        turned = source[...].T
        for h in range(heads):
            out_ref[h, offset : offset + ATT_DIM] = turned[h * ATT_DIM : (h + 1) * ATT_DIM]


def turned_rows(queries, key_rows):
    rows, width = queries.shape
    heads = width // ATT_DIM
    steps = 8
    per_step = heads // steps
    block = pl.BlockSpec((rows, width // steps), lambda i: (0, i))
    return pl.pallas_call(
        turn_kernel,
        grid=(steps,),
        in_specs=[block, block],
        out_specs=pl.BlockSpec((per_step, 2 * ATT_DIM, rows), lambda i: (i, 0, 0)),
        out_shape=jax.ShapeDtypeStruct((heads, 2 * ATT_DIM, rows), queries.dtype),
        compiler_params=PARAMS,
    )(queries, key_rows)


def scan_kernel(recv_ref, out_ref):
    blocks = recv_ref.shape[0]
    lane = lax.broadcasted_iota(jnp.int32, (LANES, PART_COLS), 0)
    column = lax.broadcasted_iota(jnp.int32, (LANES, PART_COLS), 1)
    spread = (column // HEAD_DIM == lane).astype(jnp.float32).astype(jnp.bfloat16)
    pieces = recv_ref[:, STATE_ROWS:].reshape(blocks * PART_ROWS, LANES)
    decays = jnp.dot(pieces, spread, preferred_element_type=jnp.float32)
    state = [jnp.zeros((PART_ROWS, LANES), jnp.float32) for _ in range(PART_TILES)]
    for block in range(blocks):
        decay = jnp.sum(
            decays[block * PART_ROWS : block * PART_ROWS + 8], axis=0, keepdims=True
        )
        for tile in range(PART_TILES):
            rows = slice(tile * PART_ROWS, (tile + 1) * PART_ROWS)
            out_ref[block, rows] = state[tile].astype(jnp.bfloat16)
            added = recv_ref[block, rows].astype(jnp.float32)
            state[tile] = (
                state[tile] * decay[:, tile * LANES : (tile + 1) * LANES] + added
            )


def packed_state(local_state, block_decay):
    parts = local_state.astype(jnp.bfloat16).reshape(
        ROW_PARTS, PART_ROWS, COL_PARTS, PART_TILES, LANES
    )
    parts = parts.transpose(0, 2, 3, 1, 4).reshape(-1, STATE_ROWS, LANES)
    high = lax.reduce_precision(block_decay, 8, 7)
    middle = lax.reduce_precision(block_decay - high, 8, 7)
    low = lax.reduce_precision(block_decay - high - middle, 8, 7)
    pieces = jnp.stack([high, middle, low]).astype(jnp.bfloat16)
    pieces = pieces.reshape(3, COL_PARTS, PART_HEADS).transpose(1, 0, 2)
    pieces = jnp.pad(pieces, ((0, 0), (0, PART_ROWS - 3), (0, LANES - PART_HEADS)))
    pieces = jnp.tile(pieces, (ROW_PARTS, 1, 1))
    return jnp.concatenate([parts, pieces], axis=1)


def scanned(received):
    return pl.pallas_call(
        scan_kernel,
        out_shape=jax.ShapeDtypeStruct((received.shape[0], STATE_ROWS, LANES), jnp.bfloat16),
        compiler_params=PARAMS,
    )(received)


def norm_kernel(readout_ref, state_ref, base_ref, factor_ref, gain_ref, out_ref, turned_ref, held):
    group, chunk = pl.program_id(0), pl.program_id(1)
    chunks = held.shape[0]
    readout = jnp.where(group == 0, readout_ref[:, :STATE], readout_ref[:, STATE:])
    tiles = []
    for tile in range(PART_TILES):
        rows = slice(tile * PART_ROWS, (tile + 1) * PART_ROWS)
        tiles.append(
            jnp.concatenate([state_ref[part, 0, rows] for part in range(ROW_PARTS)], axis=0)
        )
    state = jnp.concatenate(tiles, axis=1)
    across = jnp.dot(readout, state, preferred_element_type=jnp.float32)
    held[chunk] = base_ref[...] + across * factor_ref[...]

    @pl.when(chunk == chunks - 1)
    def _():
        total = jnp.zeros((held.shape[1], 1), jnp.float32)
        for c in range(chunks):
            total = total + jnp.sum(held[c] * held[c], axis=1, keepdims=True)
        scale = lax.rsqrt(total / SHARE + eps)
        per_chunk = PART_COLS // ATT_DIM
        for c in range(chunks):
            columns = slice(c * PART_COLS, (c + 1) * PART_COLS)
            normed = (held[c] * scale * gain_ref[:, columns]).astype(jnp.bfloat16)
            out_ref[:, columns] = normed
            turned = normed.T
            for h in range(per_chunk):
                turned_ref[c * per_chunk + h] = turned[h * ATT_DIM : (h + 1) * ATT_DIM]


def normed_output(readout, state_in, base, factor, norm_gain):
    rows = base.shape[0]
    chunks = COL_PARTS // GROUPS
    state_in = state_in.reshape(ROW_PARTS, COL_PARTS, STATE_ROWS, LANES)
    wide = pl.BlockSpec((rows, PART_COLS), lambda g, c: (0, g * chunks + c))
    heads = INNER // ATT_DIM // GROUPS
    return pl.pallas_call(
        norm_kernel,
        grid=(GROUPS, chunks),
        in_specs=[
            pl.BlockSpec((rows, GROUPS * STATE), lambda g, c: (0, 0)),
            pl.BlockSpec(
                (ROW_PARTS, 1, STATE_ROWS, LANES), lambda g, c: (0, g * chunks + c, 0, 0)
            ),
            wide,
            wide,
            pl.BlockSpec((1, SHARE), lambda g, c: (0, g)),
        ],
        out_specs=[
            pl.BlockSpec((rows, SHARE), lambda g, c: (0, g)),
            pl.BlockSpec((heads, ATT_DIM, rows), lambda g, c: (g, 0, 0)),
        ],
        out_shape=[
            jax.ShapeDtypeStruct((rows, INNER), jnp.bfloat16),
            jax.ShapeDtypeStruct((GROUPS * heads, ATT_DIM, rows), jnp.bfloat16),
        ],
        scratch_shapes=[pltpu.VMEM((chunks, rows, PART_COLS), jnp.float32)],
        compiler_params=PARAMS,
    )(readout, state_in, base, factor, norm_gain.reshape(1, INNER))


def weight_kernel(query_ref, key_ref, out_ref, keys, scores):
    step = pl.program_id(0)
    sources, _, rows = key_ref.shape

    @pl.when(step == 0)
    def _():
        for source in range(sources):
            keys[source * rows : (source + 1) * rows] = key_ref[source, ATT_DIM:].T

    queries = jnp.concatenate([query_ref[b] for b in range(query_ref.shape[0])], axis=1)
    chunks = (step + KEY_BLOCK // QUERY_BLOCK) // (KEY_BLOCK // QUERY_BLOCK)
    score_scale = 1.0 / math.sqrt(ATT_DIM)

    def raw(chunk):
        part = keys[pl.ds(pl.multiple_of(chunk * KEY_BLOCK, KEY_BLOCK), KEY_BLOCK)]
        return jnp.dot(part, queries, preferred_element_type=jnp.float32) * score_scale

    def slots(chunk):
        return pl.ds(pl.multiple_of(chunk * KEY_BLOCK, KEY_BLOCK), KEY_BLOCK)

    def first(chunk, top):
        values = raw(chunk)
        scores[slots(chunk)] = values
        return jnp.maximum(top, jnp.max(values.reshape(-1, 8, QUERY_BLOCK), axis=0))

    top = jnp.full((8, QUERY_BLOCK), -jnp.inf, jnp.float32)
    top = lax.fori_loop(0, chunks - 1, first, top)
    last = chunks - 1
    key_pos = last * KEY_BLOCK + lax.broadcasted_iota(jnp.int32, (KEY_BLOCK, QUERY_BLOCK), 0)
    query_pos = step * QUERY_BLOCK + lax.broadcasted_iota(
        jnp.int32, (KEY_BLOCK, QUERY_BLOCK), 1
    )
    values = jnp.where(key_pos <= query_pos, raw(last), -jnp.inf)
    scores[slots(last)] = values
    top = jnp.maximum(top, jnp.max(values.reshape(-1, 8, QUERY_BLOCK), axis=0))
    top = jnp.max(top, axis=0, keepdims=True)

    def second(chunk, total):
        values = jnp.exp(scores[slots(chunk)] - top)
        scores[slots(chunk)] = values
        return total + jnp.sum(values.reshape(-1, 8, QUERY_BLOCK), axis=0)

    total = lax.fori_loop(0, chunks, second, jnp.zeros((8, QUERY_BLOCK), jnp.float32))
    inverse = 1.0 / jnp.sum(total, axis=0, keepdims=True)

    def third(chunk, carry):
        out_ref[0, slots(chunk)] = (scores[slots(chunk)] * inverse).astype(jnp.bfloat16)
        return carry

    lax.fori_loop(0, chunks, third, 0)


def attention_weights(received):
    sources, _, rows = received.shape
    total = sources * rows
    steps = total // QUERY_BLOCK
    per_step = QUERY_BLOCK // rows
    return pl.pallas_call(
        weight_kernel,
        grid=(steps,),
        in_specs=[
            pl.BlockSpec((per_step, ATT_DIM, rows), lambda i: (i, 0, 0)),
            pl.BlockSpec((sources, 2 * ATT_DIM, rows), lambda i: (0, 0, 0)),
        ],
        out_specs=pl.BlockSpec((1, total, QUERY_BLOCK), lambda i: (i, 0, 0)),
        out_shape=jax.ShapeDtypeStruct((steps, total, QUERY_BLOCK), jnp.bfloat16),
        scratch_shapes=[
            pltpu.VMEM((total, ATT_DIM), jnp.bfloat16),
            pltpu.VMEM((total, QUERY_BLOCK), jnp.float32),
        ],
        compiler_params=PARAMS,
    )(received, received)


def mix_kernel(block_ref, chunk_ref, value_ref, weight_ref, out_ref, total):
    step = pl.program_id(0)
    chunk = chunk_ref[step]
    per_chunk = KEY_BLOCK // value_ref.shape[2]
    values = jnp.concatenate([value_ref[chunk * per_chunk + b] for b in range(per_chunk)], axis=1)
    product = jnp.dot(values, weight_ref[0], preferred_element_type=jnp.float32)

    @pl.when(chunk == 0)
    def _():
        total[...] = product

    @pl.when(chunk > 0)
    def _():
        total[...] += product

    @pl.when(chunk == block_ref[step] // (KEY_BLOCK // QUERY_BLOCK))
    def _():
        rows = out_ref.shape[2]
        for b in range(out_ref.shape[0]):
            out_ref[b] = total[:, b * rows : (b + 1) * rows].astype(jnp.bfloat16)


def mixed(weights, values):
    steps, total, _ = weights.shape
    sources, _, rows = values.shape
    pairs = [
        (i, c) for i in range(steps) for c in range(i * QUERY_BLOCK // KEY_BLOCK + 1)
    ]
    blocks = jnp.array([i for i, _ in pairs], jnp.int32)
    chunks = jnp.array([c for _, c in pairs], jnp.int32)
    return pl.pallas_call(
        mix_kernel,
        grid_spec=pltpu.PrefetchScalarGridSpec(
            num_scalar_prefetch=2,
            grid=(len(pairs),),
            in_specs=[
                pl.BlockSpec((sources, ATT_DIM, rows), lambda s, b, c: (0, 0, 0)),
                pl.BlockSpec((1, KEY_BLOCK, QUERY_BLOCK), lambda s, b, c: (b[s], c[s], 0)),
            ],
            out_specs=pl.BlockSpec(
                (QUERY_BLOCK // rows, ATT_DIM, rows), lambda s, b, c: (b[s], 0, 0)
            ),
            scratch_shapes=[pltpu.VMEM((ATT_DIM, QUERY_BLOCK), jnp.float32)],
        ),
        out_shape=jax.ShapeDtypeStruct((sources, ATT_DIM, rows), jnp.bfloat16),
        compiler_params=PARAMS,
    )(blocks, chunks, values, weights)


def local(
    conv_input,
    gate_input,
    step_raw,
    step_bias,
    decay_log,
    skip_weight,
    conv_weight,
    conv_bias,
    norm_gain,
    queries,
    key_rows,
):
    row_count = conv_input.shape[0]
    share = HEADS // GROUPS
    before = shifted(conv_input[row_count - (CONV - 1) :], "ctx", 1)
    received = exchanged(turned_rows(queries, key_rows))

    padded = jnp.concatenate([before.astype(jnp.float32), conv_input.astype(jnp.float32)], axis=0)
    inputs = convolve(padded, conv_weight, conv_bias, row_count)
    step_rates = jnp.minimum(jax.nn.softplus(step_raw + step_bias[None, :]), dt_cap)
    decay_rate = -jnp.exp(decay_log)
    running = jnp.cumsum(step_rates * decay_rate[None], axis=0)
    values = inputs[:, :INNER].astype(jnp.float32)
    writes = inputs[:, INNER : INNER + GROUPS * STATE].reshape(row_count, GROUPS, STATE)
    readout_low = inputs[:, INNER + GROUPS * STATE :]
    readout = readout_low.reshape(row_count, GROUPS, STATE)
    carry_weight = jnp.exp(running[-1][None] - running) * step_rates
    weighted = values * per_channel(carry_weight)
    local_state = jnp.concatenate(
        [
            jnp.einsum(
                "sn,sc->nc",
                writes[:, g].astype(jnp.float32),
                weighted[:, g * SHARE : (g + 1) * SHARE],
                precision=HIGHEST,
            )
            for g in range(GROUPS)
        ],
        axis=1,
    )
    parts = packed_state(local_state, jnp.exp(running[-1]))
    received, parts = lax.optimization_barrier((received, parts))
    state_in = exchanged(scanned(exchanged(parts)))

    running_heads = running.T.reshape(GROUPS, share, row_count)
    rates_heads = step_rates.T.reshape(GROUPS, share, row_count)
    positions = jnp.arange(row_count, dtype=jnp.int32)
    causal = (positions[:, None] >= positions[None, :])[None, None]
    spread = running_heads[:, :, :, None] - running_heads[:, :, None, :]
    fading = jnp.exp(jnp.where(causal, spread, -jnp.inf))
    intersection = jnp.einsum("tgn,sgn->gts", readout, writes, preferred_element_type=jnp.float32)
    mixing = intersection[:, None] * fading * rates_heads[:, :, None, :]
    grouped = values.reshape(row_count, GROUPS, share, HEAD_DIM)
    inside = jnp.einsum("gkts,sgkp->tgkp", mixing, grouped, precision=HIGHEST)
    gate = jax.nn.silu(gate_input.astype(jnp.float32))
    base = (inside.reshape(row_count, INNER) + per_channel(skip_weight)[None] * values) * gate
    factor = per_channel(jnp.exp(running)) * gate

    mamba_out, turned_out = normed_output(readout_low, state_in, base, factor, norm_gain)
    weights = attention_weights(received)
    attended_heads = mixed(weights, exchanged(turned_out))
    attended = exchanged(attended_heads)
    attended = attended.transpose(2, 0, 1).reshape(row_count, INNER)
    return (mamba_out, attended)


def solution(mesh):
    rows = P(("dp", "ctx"), None)
    placed = (rows, rows, rows, P(), P(), P(), P(), P(), P(), rows, rows)
    return jax.shard_map(
        local, mesh=mesh, in_specs=placed, out_specs=(rows, rows), check_vma=False
    )
```

```python
import functools
import math

import jax
import jax.numpy as jnp
from jax import lax
from jax.experimental import pallas as pl
from jax.experimental.pallas import tpu as pltpu
from jax.sharding import PartitionSpec as P

HEADS = 112
HEAD_DIM = 64
STATE = 64
GROUPS = 2
CONV = 4
ATT_DIM = 224
INNER = HEADS * HEAD_DIM
SHARE = INNER // GROUPS

ROW_PARTS = 4
COL_PARTS = 8
PART_ROWS = STATE // ROW_PARTS
PART_COLS = INNER // COL_PARTS
LANES = 128
PART_TILES = PART_COLS // LANES
PART_HEADS = PART_COLS // HEAD_DIM
STATE_ROWS = PART_TILES * PART_ROWS

BLOCK = 1024
HALF = BLOCK // 2
PADDED = 256
NEAR = ROW_PARTS

dt_cap = 3.0
eps = 1e-05
HIGHEST = lax.Precision.HIGHEST
VMEM_LIMIT = 48 * 1024 * 1024
PARAMS = pltpu.CompilerParams(vmem_limit_bytes=VMEM_LIMIT)
SMALL_PARAMS = pltpu.CompilerParams(vmem_limit_bytes=VMEM_LIMIT // 2)


def far_size():
    return lax.axis_size("ctx") // NEAR


def shifted(array, axis, by):
    size = lax.axis_size(axis)
    pairs = [(i, i + by) for i in range(size) if 0 <= i + by < size]
    return lax.ppermute(array, axis, pairs)


def near_shifted(array, by):
    pairs = [
        (far * NEAR + near, far * NEAR + (near + by) % NEAR)
        for far in range(far_size())
        for near in range(NEAR)
    ]
    return lax.ppermute(array, "ctx", pairs)


def exchanged(array):
    return lax.all_to_all(array, "ctx", 0, 0, tiled=True)


def far_exchanged(array):
    groups = [[far * NEAR + near for far in range(far_size())] for near in range(NEAR)]
    return lax.all_to_all(array, "ctx", 0, 0, axis_index_groups=groups, tiled=True)


def convolve(padded, conv_weight, conv_bias, row_count):
    total = conv_bias[None, :] + conv_weight[0][None, :] * padded[0:row_count]
    for tap_index in range(1, conv_weight.shape[0]):
        total = total + conv_weight[tap_index][None, :] * padded[tap_index : tap_index + row_count]
    return jax.nn.silu(total).astype(jnp.bfloat16)


def head_columns(first, count):
    head = lax.broadcasted_iota(jnp.int32, (LANES, count), 0)
    channel = lax.broadcasted_iota(jnp.int32, (LANES, count), 1) + first
    return (channel // HEAD_DIM == head).astype(jnp.float32).astype(jnp.bfloat16)


def pieces_of(value):
    high = value.astype(jnp.bfloat16)
    rest = value - high.astype(jnp.float32)
    middle = rest.astype(jnp.bfloat16)
    low = (rest - middle.astype(jnp.float32)).astype(jnp.bfloat16)
    return high, middle, low


def per_channel(by_head):
    heads = jnp.arange(HEADS)[:, None]
    channels = jnp.arange(INNER)[None, :] // HEAD_DIM
    return jnp.dot(by_head, (heads == channels).astype(jnp.float32), precision=HIGHEST)


def turn_kernel(source_ref, out_ref):
    turned = source_ref[...].T
    for h in range(out_ref.shape[0]):
        out_ref[h] = turned[h * ATT_DIM : (h + 1) * ATT_DIM]


def turned_rows(source):
    rows, width = source.shape
    heads = width // ATT_DIM
    steps = 2
    return pl.pallas_call(
        turn_kernel,
        grid=(steps,),
        in_specs=[pl.BlockSpec((rows, width // steps), lambda i: (0, i))],
        out_specs=pl.BlockSpec((heads // steps, ATT_DIM, rows), lambda i: (i, 0, 0)),
        out_shape=jax.ShapeDtypeStruct((heads, ATT_DIM, rows), source.dtype),
        compiler_params=PARAMS,
    )(source)


PART_LINES = STATE_ROWS + PART_ROWS


def rounded_rows(values):
    rows = [piece.astype(jnp.float32) for piece in pieces_of(values)]
    rows.append(jnp.zeros((PART_ROWS - 3, LANES), jnp.float32))
    return jnp.concatenate(rows, axis=0).astype(jnp.bfloat16)


def state_kernel(near_ref, input_ref, write_ref, carry_ref, decay_ref, out_ref, state):
    step = pl.program_id(0)
    per_step = out_ref.shape[1]
    decays = rounded_rows(decay_ref[...])
    carry = pieces_of(carry_ref[...])
    for c in range(per_step):
        columns = head_columns((step * per_step + c) * PART_COLS, PART_COLS)
        spread = sum(jnp.dot(p, columns, preferred_element_type=jnp.float32) for p in carry)
        source = input_ref[:, c * PART_COLS : (c + 1) * PART_COLS].astype(jnp.float32)
        weighted = source * spread
        high = weighted.astype(jnp.bfloat16)
        low = (weighted - high.astype(jnp.float32)).astype(jnp.bfloat16)
        state[...] = jnp.dot(write_ref[...], high, preferred_element_type=jnp.float32) + jnp.dot(
            write_ref[...], low, preferred_element_type=jnp.float32
        )
        for r in range(NEAR):
            part = lax.rem(near_ref[0] + r, NEAR)
            rows = state[pl.ds(pl.multiple_of(part * PART_ROWS, PART_ROWS), PART_ROWS)]
            rows = rows.astype(jnp.bfloat16)
            for tile in range(PART_TILES):
                out_ref[r, c, tile * PART_ROWS : (tile + 1) * PART_ROWS] = rows[
                    :, tile * LANES : (tile + 1) * LANES
                ]
            out_ref[r, c, STATE_ROWS:] = decays


def block_states(near, inputs, writes, carry, decay):
    rows = inputs.shape[0]
    steps = 4
    per_step = COL_PARTS // steps
    padding = ((0, 0), (0, LANES - HEADS))
    whole = pl.BlockSpec(memory_space=pltpu.SMEM)
    return pl.pallas_call(
        state_kernel,
        grid=(steps,),
        in_specs=[
            whole,
            pl.BlockSpec((rows, per_step * PART_COLS), lambda i: (0, i)),
            pl.BlockSpec((STATE, rows), lambda i: (i // (steps // GROUPS), 0)),
            pl.BlockSpec((rows, LANES), lambda i: (0, 0)),
            pl.BlockSpec((1, LANES), lambda i: (0, 0)),
        ],
        out_specs=pl.BlockSpec((NEAR, per_step, PART_LINES, LANES), lambda i: (0, i, 0, 0)),
        out_shape=jax.ShapeDtypeStruct((NEAR, COL_PARTS, PART_LINES, LANES), jnp.bfloat16),
        scratch_shapes=[pltpu.VMEM((STATE, PART_COLS), jnp.float32)],
        compiler_params=PARAMS,
    )(near, inputs, writes.T, jnp.pad(carry, padding), jnp.pad(decay[None], padding))


def decay_row(part):
    lines = part[STATE_ROWS : STATE_ROWS + 8].astype(jnp.float32)
    return jnp.sum(lines, axis=0, keepdims=True)


def spread_decay(part, columns):
    spread = jnp.dot(part[STATE_ROWS:], columns, preferred_element_type=jnp.float32)
    return jnp.sum(spread[:8], axis=0, keepdims=True)


def advanced(state, part, columns):
    decay = spread_decay(part, columns)
    return [
        state[t] * decay[:, t * LANES : (t + 1) * LANES]
        + part[t * PART_ROWS : (t + 1) * PART_ROWS].astype(jnp.float32)
        for t in range(PART_TILES)
    ]


def no_state():
    return [jnp.zeros((PART_ROWS, LANES), jnp.float32) for _ in range(PART_TILES)]


def in_order(near_ref, refs, ordered):
    for r in range(NEAR):
        ordered[lax.rem(near_ref[0] + NEAR - r, NEAR)] = refs[r][...]


def group_kernel(near_ref, *refs):
    out_ref, ordered = refs[NEAR:]
    in_order(near_ref, refs[:NEAR], ordered)
    decay = decay_row(ordered[0, 0])
    for near in range(1, NEAR):
        decay = decay * decay_row(ordered[near, 0])
    decays = rounded_rows(decay)
    for c in range(COL_PARTS):
        columns = head_columns(c * PART_COLS, PART_COLS)
        state = no_state()
        for near in range(NEAR):
            state = advanced(state, ordered[near, c], columns)
        for t in range(PART_TILES):
            out_ref[c, t * PART_ROWS : (t + 1) * PART_ROWS] = state[t].astype(jnp.bfloat16)
        out_ref[c, STATE_ROWS:] = decays


def group_state(near, parts):
    vmem = pl.BlockSpec(memory_space=pltpu.VMEM)
    return pl.pallas_call(
        group_kernel,
        in_specs=[pl.BlockSpec(memory_space=pltpu.SMEM)] + [vmem] * NEAR,
        out_specs=vmem,
        out_shape=jax.ShapeDtypeStruct(parts[0].shape, jnp.bfloat16),
        scratch_shapes=[pltpu.VMEM((NEAR,) + parts[0].shape, jnp.bfloat16)],
        compiler_params=PARAMS,
    )(near, *parts)


def scan_kernel(far_ref, recv_ref, out_ref):
    columns = head_columns(far_ref[0] * PART_COLS, PART_COLS)
    groups = recv_ref.shape[0]
    state = no_state()
    for group in range(groups):
        for t in range(PART_TILES):
            rows = slice(t * PART_ROWS, (t + 1) * PART_ROWS)
            out_ref[group, rows] = state[t].astype(jnp.bfloat16)
        if group < groups - 1:
            state = advanced(state, recv_ref[group], columns)


def scanned(far, received):
    vmem = pl.BlockSpec(memory_space=pltpu.VMEM)
    return pl.pallas_call(
        scan_kernel,
        in_specs=[pl.BlockSpec(memory_space=pltpu.SMEM), vmem],
        out_specs=vmem,
        out_shape=jax.ShapeDtypeStruct((received.shape[0], STATE_ROWS, LANES), jnp.bfloat16),
        compiler_params=PARAMS,
    )(far, received)


def enter_kernel(near_ref, *refs):
    group_ref, out_ref, ordered = refs[NEAR:]
    in_order(near_ref, refs[:NEAR], ordered)
    for c in range(COL_PARTS):
        columns = head_columns(c * PART_COLS, PART_COLS)
        state = [
            group_ref[c, t * PART_ROWS : (t + 1) * PART_ROWS].astype(jnp.float32)
            for t in range(PART_TILES)
        ]
        for near in range(NEAR):
            place = lax.rem(near - near_ref[0] + NEAR, NEAR)
            for t in range(PART_TILES):
                out_ref[place, c, t * PART_ROWS : (t + 1) * PART_ROWS] = state[t].astype(
                    jnp.bfloat16
                )
            if near < NEAR - 1:
                state = advanced(state, ordered[near, c], columns)


def entering_states(near, parts, group_in):
    vmem = pl.BlockSpec(memory_space=pltpu.VMEM)
    return pl.pallas_call(
        enter_kernel,
        in_specs=[pl.BlockSpec(memory_space=pltpu.SMEM)] + [vmem] * (NEAR + 1),
        out_specs=vmem,
        out_shape=jax.ShapeDtypeStruct((NEAR, COL_PARTS, STATE_ROWS, LANES), jnp.bfloat16),
        scratch_shapes=[pltpu.VMEM((NEAR,) + parts[0].shape, jnp.bfloat16)],
        compiler_params=PARAMS,
    )(near, *parts, group_in)


def norm_kernel(readout_ref, *refs):
    states = refs[:NEAR]
    base_ref, factor_ref, gain_ref, out_ref, turned_ref = refs[NEAR:]
    readout = readout_ref[0]
    held = []
    total = 0.0
    chunks = out_ref.shape[1] // PART_COLS
    for c in range(chunks):
        columns = slice(c * PART_COLS, (c + 1) * PART_COLS)
        tiles = []
        for tile in range(PART_TILES):
            rows = slice(tile * PART_ROWS, (tile + 1) * PART_ROWS)
            tiles.append(jnp.concatenate([state[c, rows] for state in states], axis=0))
        state = jnp.concatenate(tiles, axis=1)
        across = jnp.dot(readout, state, preferred_element_type=jnp.float32)
        values = base_ref[:, columns] + across * factor_ref[:, columns]
        held.append(values)
        total = total + jnp.sum(values * values, axis=1, keepdims=True)
    scale = lax.rsqrt(total / SHARE + eps)
    per_chunk = PART_COLS // ATT_DIM
    for c in range(chunks):
        columns = slice(c * PART_COLS, (c + 1) * PART_COLS)
        normed = (held[c] * scale * gain_ref[:, columns]).astype(jnp.bfloat16)
        out_ref[:, columns] = normed
        turned = normed.T
        for h in range(per_chunk):
            turned_ref[c * per_chunk + h] = turned[h * ATT_DIM : (h + 1) * ATT_DIM]


def normed_output(readout, states, base, factor, norm_gain):
    rows = base.shape[0]
    chunks = COL_PARTS // GROUPS
    wide = pl.BlockSpec((rows, SHARE), lambda g: (0, g))
    heads = INNER // ATT_DIM // GROUPS
    part = pl.BlockSpec((chunks, STATE_ROWS, LANES), lambda g: (g, 0, 0))
    return pl.pallas_call(
        norm_kernel,
        grid=(GROUPS,),
        in_specs=[pl.BlockSpec((1, rows, STATE), lambda g: (g, 0, 0))]
        + [part] * NEAR
        + [wide, wide, pl.BlockSpec((1, SHARE), lambda g: (0, g))],
        out_specs=[wide, pl.BlockSpec((heads, ATT_DIM, rows), lambda g: (g, 0, 0))],
        out_shape=[
            jax.ShapeDtypeStruct((rows, INNER), jnp.bfloat16),
            jax.ShapeDtypeStruct((GROUPS * heads, ATT_DIM, rows), jnp.bfloat16),
        ],
        compiler_params=PARAMS,
    )(readout, *states, base, factor, norm_gain.reshape(1, INNER))


def weight_pieces(total):
    pieces = []
    for i in range(total // BLOCK):
        pieces += [(i, c, 0, BLOCK, BLOCK) for c in range(i)]
        pieces += [(i, i, 0, HALF, HALF), (i, i, HALF, HALF, BLOCK)]
    return pieces


def folded(values, combine):
    result = values[:, :LANES]
    for b in range(1, values.shape[1] // LANES):
        result = combine(result, values[:, b * LANES : (b + 1) * LANES])
    return result


def joined(source_ref, start):
    rows = source_ref.shape[2]
    blocks = [source_ref[start // rows + b] for b in range(HALF // rows)]
    return jnp.concatenate(blocks, axis=1)


def weight_kernel(query_ref, key_ref, *refs):
    scores = refs[-1]
    total = query_ref.shape[0] * query_ref.shape[2]
    places = {piece[:3]: ref for piece, ref in zip(weight_pieces(total), refs)}
    score_scale = 1.0 / math.sqrt(ATT_DIM)
    for start in range(0, total, HALF):
        block, offset = start // BLOCK, start % BLOCK
        queries = joined(query_ref, start).T
        spans = [slice(c, c + HALF) for c in range(0, start + HALF, HALF)]
        top = None
        for span in spans:
            values = (
                jnp.dot(queries, joined(key_ref, span.start), preferred_element_type=jnp.float32)
                * score_scale
            )
            if span.start == start:
                query_pos = lax.broadcasted_iota(jnp.int32, values.shape, 0)
                key_pos = lax.broadcasted_iota(jnp.int32, values.shape, 1)
                values = jnp.where(key_pos <= query_pos, values, -jnp.inf)
            scores[:, span] = values
            part = folded(values, jnp.maximum)
            top = part if top is None else jnp.maximum(top, part)
        top = jnp.max(top, axis=1, keepdims=True)
        norm = 0.0
        for span in spans:
            values = jnp.exp(scores[:, span] - top)
            scores[:, span] = values
            norm = norm + folded(values, jnp.add)
        inverse = 1.0 / jnp.sum(norm, axis=1, keepdims=True)
        for span in spans:
            values = (scores[:, span] * inverse).astype(jnp.bfloat16)
            other, column = span.start // BLOCK, span.start % BLOCK
            columns = slice(column, column + HALF)
            if other < block:
                places[block, other, 0][offset : offset + HALF, columns] = values
            else:
                places[block, block, offset][:, columns] = values


def attention_weights(queries, keys):
    sources, _, rows = keys.shape
    pieces = weight_pieces(sources * rows)
    vmem = pl.BlockSpec(memory_space=pltpu.VMEM)
    return pl.pallas_call(
        weight_kernel,
        in_specs=[vmem] * 2,
        out_specs=[vmem] * len(pieces),
        out_shape=[pltpu.VMEM((count, span), jnp.bfloat16) for _, _, _, count, span in pieces],
        scratch_shapes=[pltpu.VMEM((HALF, sources * rows), jnp.float32)],
        compiler_params=SMALL_PARAMS,
    )(queries, keys)


def mix_kernel(value_ref, *refs):
    out_ref, values = refs[-2:]
    rows = value_ref.shape[2]
    total = value_ref.shape[0] * rows
    per_block = BLOCK // rows
    padding = jnp.zeros((PADDED - ATT_DIM, rows), jnp.bfloat16)
    for b in range(value_ref.shape[0]):
        padded = jnp.concatenate([value_ref[b], padding], axis=0)
        values[b * rows : (b + 1) * rows] = padded.T
    before = 0.0
    for (i, c, start, count, span), weights in zip(weight_pieces(total), refs):
        part = values[c * BLOCK : c * BLOCK + span]
        product = jnp.dot(weights[...], part, preferred_element_type=jnp.float32)
        if c < i:
            before = product + before
            continue
        if i > 0:
            product = product + before[start : start + count]
        result = product.astype(jnp.bfloat16)
        for b in range(count // rows):
            turned = result[b * rows : (b + 1) * rows].T
            out_ref[i * per_block + start // rows + b] = turned[:ATT_DIM]
        if start > 0:
            before = 0.0


def mixed(weights, values):
    sources, _, rows = values.shape
    vmem = pl.BlockSpec(memory_space=pltpu.VMEM)
    return pl.pallas_call(
        mix_kernel,
        in_specs=[vmem] * (1 + len(weights)),
        out_specs=vmem,
        out_shape=jax.ShapeDtypeStruct((sources, ATT_DIM, rows), jnp.bfloat16),
        scratch_shapes=[pltpu.VMEM((sources * rows, PADDED), jnp.bfloat16)],
        compiler_params=SMALL_PARAMS,
    )(values, *weights)


def local(
    conv_input,
    gate_input,
    step_raw,
    step_bias,
    decay_log,
    skip_weight,
    conv_weight,
    conv_bias,
    norm_gain,
    queries,
    key_rows,
):
    row_count = conv_input.shape[0]
    share = HEADS // GROUPS
    before = shifted(conv_input[row_count - (CONV - 1) :], "ctx", 1)
    head_queries = exchanged(turned_rows(queries))

    padded = jnp.concatenate([before.astype(jnp.float32), conv_input.astype(jnp.float32)], axis=0)
    inputs = convolve(padded, conv_weight, conv_bias, row_count)
    step_rates = jnp.minimum(jax.nn.softplus(step_raw + step_bias[None, :]), dt_cap)
    decay_rate = -jnp.exp(decay_log)
    running = jnp.cumsum(step_rates * decay_rate[None], axis=0)
    values = inputs[:, :INNER].astype(jnp.float32)
    writes = inputs[:, INNER : INNER + GROUPS * STATE].reshape(row_count, GROUPS, STATE)
    readout_low = inputs[:, INNER + GROUPS * STATE :]
    readout = readout_low.reshape(row_count, GROUPS, STATE)
    carry_weight = jnp.exp(running[-1][None] - running) * step_rates
    near = lax.rem(lax.axis_index("ctx"), NEAR)
    parts = block_states(
        near[None],
        inputs,
        inputs[:, INNER : INNER + GROUPS * STATE],
        carry_weight,
        jnp.exp(running[-1]),
    )
    running_heads = running.T.reshape(GROUPS, share, row_count)
    rates_heads = step_rates.T.reshape(GROUPS, share, row_count)
    positions = jnp.arange(row_count, dtype=jnp.int32)
    causal = (positions[:, None] >= positions[None, :])[None, None]
    spread = running_heads[:, :, :, None] - running_heads[:, :, None, :]
    fading = jnp.exp(jnp.where(causal, spread, -jnp.inf))
    intersection = jnp.einsum("tgn,sgn->gts", readout, writes, preferred_element_type=jnp.float32)
    mixing = intersection[:, None] * fading * rates_heads[:, :, None, :]
    grouped = values.reshape(row_count, GROUPS, share, HEAD_DIM)
    inside = jnp.einsum("gkts,sgkp->tgkp", mixing, grouped, precision=HIGHEST)

    parts = [parts[0]] + [near_shifted(parts[r], r) for r in range(1, NEAR)]
    inside, *parts = lax.optimization_barrier((inside, *parts))
    total = group_state(near[None], parts)
    head_queries, total = lax.optimization_barrier((head_queries, total))
    far = lax.axis_index("ctx") // NEAR
    group_in = far_exchanged(scanned(far[None], far_exchanged(total)))
    turned_keys, group_in = lax.optimization_barrier((turned_rows(key_rows), group_in))
    head_keys = exchanged(turned_keys)
    entering = entering_states(near[None], parts, group_in)
    states = [entering[0]] + [near_shifted(entering[r], r) for r in range(1, NEAR)]
    order = lax.rem(near + NEAR - jnp.arange(NEAR), NEAR)
    readout_parts = readout_low.reshape(row_count, GROUPS, ROW_PARTS, PART_ROWS)
    readout_parts = jnp.take(readout_parts, order, axis=2).reshape(row_count, GROUPS, STATE)
    readout_parts = readout_parts.transpose(1, 0, 2)

    gate = jax.nn.silu(gate_input.astype(jnp.float32))
    base = (inside.reshape(row_count, INNER) + per_channel(skip_weight)[None] * values) * gate
    factor = per_channel(jnp.exp(running)) * gate

    mamba_out, turned_out = normed_output(readout_parts, states, base, factor, norm_gain)
    weights = attention_weights(head_queries, head_keys)
    attended_heads = mixed(weights, exchanged(turned_out))
    attended = exchanged(attended_heads)
    attended = attended.transpose(2, 0, 1).reshape(row_count, INNER)
    return (mamba_out, attended)


def solution(mesh):
    rows = P(("dp", "ctx"), None)
    placed = (rows, rows, rows, P(), P(), P(), P(), P(), P(), rows, rows)
    return jax.shard_map(
        local, mesh=mesh, in_specs=placed, out_specs=(rows, rows), check_vma=False
    )
```

```python
import functools
import math

import jax
import jax.numpy as jnp
from jax import lax
from jax.experimental import pallas as pl
from jax.experimental.pallas import tpu as pltpu
from jax.sharding import PartitionSpec as P

HEADS = 112
HEAD_DIM = 64
STATE = 64
GROUPS = 2
CONV = 4
ATT_DIM = 224
INNER = HEADS * HEAD_DIM
SHARE = INNER // GROUPS

ROW_PARTS = 4
COL_PARTS = 8
PART_ROWS = STATE // ROW_PARTS
PART_COLS = INNER // COL_PARTS
LANES = 128
PART_TILES = PART_COLS // LANES
PART_HEADS = PART_COLS // HEAD_DIM
STATE_ROWS = PART_TILES * PART_ROWS

BLOCK = 1024
HALF = BLOCK // 2
STRIP = 256
PADDED = 256
NEAR = ROW_PARTS

dt_cap = 3.0
eps = 1e-05
HIGHEST = lax.Precision.HIGHEST
VMEM_LIMIT = 48 * 1024 * 1024
PARAMS = pltpu.CompilerParams(vmem_limit_bytes=VMEM_LIMIT)


def far_size():
    return lax.axis_size("ctx") // NEAR


def shifted(array, axis, by):
    size = lax.axis_size(axis)
    pairs = [(i, i + by) for i in range(size) if 0 <= i + by < size]
    return lax.ppermute(array, axis, pairs)


def near_shifted(array, by):
    pairs = [
        (far * NEAR + near, far * NEAR + (near + by) % NEAR)
        for far in range(far_size())
        for near in range(NEAR)
    ]
    return lax.ppermute(array, "ctx", pairs)


def exchanged(array):
    return lax.all_to_all(array, "ctx", 0, 0, tiled=True)


def far_exchanged(array):
    groups = [[far * NEAR + near for far in range(far_size())] for near in range(NEAR)]
    return lax.all_to_all(array, "ctx", 0, 0, axis_index_groups=groups, tiled=True)


def convolve(padded, conv_weight, conv_bias, row_count):
    total = conv_bias[None, :] + conv_weight[0][None, :] * padded[0:row_count]
    for tap_index in range(1, conv_weight.shape[0]):
        total = total + conv_weight[tap_index][None, :] * padded[tap_index : tap_index + row_count]
    return jax.nn.silu(total).astype(jnp.bfloat16)


def head_columns(first, count):
    head = lax.broadcasted_iota(jnp.int32, (LANES, count), 0)
    channel = lax.broadcasted_iota(jnp.int32, (LANES, count), 1) + first
    return (channel // HEAD_DIM == head).astype(jnp.float32).astype(jnp.bfloat16)


def pieces_of(value):
    high = value.astype(jnp.bfloat16)
    rest = value - high.astype(jnp.float32)
    middle = rest.astype(jnp.bfloat16)
    low = (rest - middle.astype(jnp.float32)).astype(jnp.bfloat16)
    return high, middle, low


def per_channel(by_head):
    heads = jnp.arange(HEADS)[:, None]
    channels = jnp.arange(INNER)[None, :] // HEAD_DIM
    return jnp.dot(by_head, (heads == channels).astype(jnp.float32), precision=HIGHEST)


def turn_kernel(source_ref, out_ref):
    turned = source_ref[...].T
    for h in range(out_ref.shape[0]):
        out_ref[h] = turned[h * ATT_DIM : (h + 1) * ATT_DIM]


def turned_rows(source):
    rows, width = source.shape
    heads = width // ATT_DIM
    steps = 2
    return pl.pallas_call(
        turn_kernel,
        grid=(steps,),
        in_specs=[pl.BlockSpec((rows, width // steps), lambda i: (0, i))],
        out_specs=pl.BlockSpec((heads // steps, ATT_DIM, rows), lambda i: (i, 0, 0)),
        out_shape=jax.ShapeDtypeStruct((heads, ATT_DIM, rows), source.dtype),
        compiler_params=PARAMS,
    )(source)


PART_LINES = STATE_ROWS + PART_ROWS


def rounded_rows(values):
    rows = [piece.astype(jnp.float32) for piece in pieces_of(values)]
    rows.append(jnp.zeros((PART_ROWS - 3, LANES), jnp.float32))
    return jnp.concatenate(rows, axis=0).astype(jnp.bfloat16)


def state_kernel(near_ref, input_ref, write_ref, carry_ref, decay_ref, out_ref, state):
    step = pl.program_id(0)
    per_step = out_ref.shape[1]
    decays = rounded_rows(decay_ref[...])
    carry = pieces_of(carry_ref[...])
    for c in range(per_step):
        columns = head_columns((step * per_step + c) * PART_COLS, PART_COLS)
        spread = sum(jnp.dot(p, columns, preferred_element_type=jnp.float32) for p in carry)
        source = input_ref[:, c * PART_COLS : (c + 1) * PART_COLS].astype(jnp.float32)
        weighted = source * spread
        high = weighted.astype(jnp.bfloat16)
        low = (weighted - high.astype(jnp.float32)).astype(jnp.bfloat16)
        state[...] = jnp.dot(write_ref[...], high, preferred_element_type=jnp.float32) + jnp.dot(
            write_ref[...], low, preferred_element_type=jnp.float32
        )
        for r in range(NEAR):
            part = lax.rem(near_ref[0] + r, NEAR)
            rows = state[pl.ds(pl.multiple_of(part * PART_ROWS, PART_ROWS), PART_ROWS)]
            rows = rows.astype(jnp.bfloat16)
            for tile in range(PART_TILES):
                out_ref[r, c, tile * PART_ROWS : (tile + 1) * PART_ROWS] = rows[
                    :, tile * LANES : (tile + 1) * LANES
                ]
            out_ref[r, c, STATE_ROWS:] = decays


def block_states(near, inputs, writes, carry, decay):
    rows = inputs.shape[0]
    steps = 4
    per_step = COL_PARTS // steps
    padding = ((0, 0), (0, LANES - HEADS))
    whole = pl.BlockSpec(memory_space=pltpu.SMEM)
    return pl.pallas_call(
        state_kernel,
        grid=(steps,),
        in_specs=[
            whole,
            pl.BlockSpec((rows, per_step * PART_COLS), lambda i: (0, i)),
            pl.BlockSpec((STATE, rows), lambda i: (i // (steps // GROUPS), 0)),
            pl.BlockSpec((rows, LANES), lambda i: (0, 0)),
            pl.BlockSpec((1, LANES), lambda i: (0, 0)),
        ],
        out_specs=pl.BlockSpec((NEAR, per_step, PART_LINES, LANES), lambda i: (0, i, 0, 0)),
        out_shape=jax.ShapeDtypeStruct((NEAR, COL_PARTS, PART_LINES, LANES), jnp.bfloat16),
        scratch_shapes=[pltpu.VMEM((STATE, PART_COLS), jnp.float32)],
        compiler_params=PARAMS,
    )(near, inputs, writes.T, jnp.pad(carry, padding), jnp.pad(decay[None], padding))


def decay_row(part):
    lines = part[STATE_ROWS : STATE_ROWS + 8].astype(jnp.float32)
    return jnp.sum(lines, axis=0, keepdims=True)


def spread_decay(part, columns):
    spread = jnp.dot(part[STATE_ROWS:], columns, preferred_element_type=jnp.float32)
    return jnp.sum(spread[:8], axis=0, keepdims=True)


def advanced(state, part, columns):
    decay = spread_decay(part, columns)
    return [
        state[t] * decay[:, t * LANES : (t + 1) * LANES]
        + part[t * PART_ROWS : (t + 1) * PART_ROWS].astype(jnp.float32)
        for t in range(PART_TILES)
    ]


def no_state():
    return [jnp.zeros((PART_ROWS, LANES), jnp.float32) for _ in range(PART_TILES)]


def in_order(near_ref, refs, ordered):
    for r in range(NEAR):
        ordered[lax.rem(near_ref[0] + NEAR - r, NEAR)] = refs[r][...]


def group_kernel(near_ref, *refs):
    out_ref, ordered = refs[NEAR:]
    in_order(near_ref, refs[:NEAR], ordered)
    decay = decay_row(ordered[0, 0])
    for near in range(1, NEAR):
        decay = decay * decay_row(ordered[near, 0])
    decays = rounded_rows(decay)
    for c in range(COL_PARTS):
        columns = head_columns(c * PART_COLS, PART_COLS)
        state = no_state()
        for near in range(NEAR):
            state = advanced(state, ordered[near, c], columns)
        for t in range(PART_TILES):
            out_ref[c, t * PART_ROWS : (t + 1) * PART_ROWS] = state[t].astype(jnp.bfloat16)
        out_ref[c, STATE_ROWS:] = decays


def group_state(near, parts):
    vmem = pl.BlockSpec(memory_space=pltpu.VMEM)
    return pl.pallas_call(
        group_kernel,
        in_specs=[pl.BlockSpec(memory_space=pltpu.SMEM)] + [vmem] * NEAR,
        out_specs=vmem,
        out_shape=jax.ShapeDtypeStruct(parts[0].shape, jnp.bfloat16),
        scratch_shapes=[pltpu.VMEM((NEAR,) + parts[0].shape, jnp.bfloat16)],
        compiler_params=PARAMS,
    )(near, *parts)


def scan_kernel(far_ref, recv_ref, out_ref):
    columns = head_columns(far_ref[0] * PART_COLS, PART_COLS)
    groups = recv_ref.shape[0]
    state = no_state()
    for group in range(groups):
        for t in range(PART_TILES):
            rows = slice(t * PART_ROWS, (t + 1) * PART_ROWS)
            out_ref[group, rows] = state[t].astype(jnp.bfloat16)
        if group < groups - 1:
            state = advanced(state, recv_ref[group], columns)


def scanned(far, received):
    vmem = pl.BlockSpec(memory_space=pltpu.VMEM)
    return pl.pallas_call(
        scan_kernel,
        in_specs=[pl.BlockSpec(memory_space=pltpu.SMEM), vmem],
        out_specs=vmem,
        out_shape=jax.ShapeDtypeStruct((received.shape[0], STATE_ROWS, LANES), jnp.bfloat16),
        compiler_params=PARAMS,
    )(far, received)


def enter_kernel(near_ref, *refs):
    group_ref, out_ref, ordered = refs[NEAR:]
    in_order(near_ref, refs[:NEAR], ordered)
    for c in range(COL_PARTS):
        columns = head_columns(c * PART_COLS, PART_COLS)
        state = [
            group_ref[c, t * PART_ROWS : (t + 1) * PART_ROWS].astype(jnp.float32)
            for t in range(PART_TILES)
        ]
        for near in range(NEAR):
            place = lax.rem(near - near_ref[0] + NEAR, NEAR)
            for t in range(PART_TILES):
                out_ref[place, c, t * PART_ROWS : (t + 1) * PART_ROWS] = state[t].astype(
                    jnp.bfloat16
                )
            if near < NEAR - 1:
                state = advanced(state, ordered[near, c], columns)


def entering_states(near, parts, group_in):
    vmem = pl.BlockSpec(memory_space=pltpu.VMEM)
    return pl.pallas_call(
        enter_kernel,
        in_specs=[pl.BlockSpec(memory_space=pltpu.SMEM)] + [vmem] * (NEAR + 1),
        out_specs=vmem,
        out_shape=jax.ShapeDtypeStruct((NEAR, COL_PARTS, STATE_ROWS, LANES), jnp.bfloat16),
        scratch_shapes=[pltpu.VMEM((NEAR,) + parts[0].shape, jnp.bfloat16)],
        compiler_params=PARAMS,
    )(near, *parts, group_in)


def norm_kernel(readout_ref, *refs):
    states = refs[:NEAR]
    base_ref, factor_ref, gain_ref, out_ref, turned_ref = refs[NEAR:]
    readout = readout_ref[0]
    held = []
    total = 0.0
    chunks = out_ref.shape[1] // PART_COLS
    for c in range(chunks):
        columns = slice(c * PART_COLS, (c + 1) * PART_COLS)
        tiles = []
        for tile in range(PART_TILES):
            rows = slice(tile * PART_ROWS, (tile + 1) * PART_ROWS)
            tiles.append(jnp.concatenate([state[c, rows] for state in states], axis=0))
        state = jnp.concatenate(tiles, axis=1)
        across = jnp.dot(readout, state, preferred_element_type=jnp.float32)
        values = base_ref[:, columns] + across * factor_ref[:, columns]
        held.append(values)
        total = total + jnp.sum(values * values, axis=1, keepdims=True)
    scale = lax.rsqrt(total / SHARE + eps)
    per_chunk = PART_COLS // ATT_DIM
    for c in range(chunks):
        columns = slice(c * PART_COLS, (c + 1) * PART_COLS)
        normed = (held[c] * scale * gain_ref[:, columns]).astype(jnp.bfloat16)
        out_ref[:, columns] = normed
        turned = normed.T
        for h in range(per_chunk):
            turned_ref[c * per_chunk + h] = turned[h * ATT_DIM : (h + 1) * ATT_DIM]


def normed_output(readout, states, base, factor, norm_gain):
    rows = base.shape[0]
    chunks = COL_PARTS // GROUPS
    wide = pl.BlockSpec((rows, SHARE), lambda g: (0, g))
    heads = INNER // ATT_DIM // GROUPS
    part = pl.BlockSpec((chunks, STATE_ROWS, LANES), lambda g: (g, 0, 0))
    return pl.pallas_call(
        norm_kernel,
        grid=(GROUPS,),
        in_specs=[pl.BlockSpec((1, rows, STATE), lambda g: (g, 0, 0))]
        + [part] * NEAR
        + [wide, wide, pl.BlockSpec((1, SHARE), lambda g: (0, g))],
        out_specs=[wide, pl.BlockSpec((heads, ATT_DIM, rows), lambda g: (g, 0, 0))],
        out_shape=[
            jax.ShapeDtypeStruct((rows, INNER), jnp.bfloat16),
            jax.ShapeDtypeStruct((GROUPS * heads, ATT_DIM, rows), jnp.bfloat16),
        ],
        compiler_params=PARAMS,
    )(readout, *states, base, factor, norm_gain.reshape(1, INNER))


def weight_blocks(total):
    return [(i, c) for i in range(total // BLOCK) for c in range(i + 1)]


def weight_pieces(total):
    pieces = []
    for i in range(total // BLOCK):
        place = i * (i + 1) // 2
        row = [(place + c, c, 0, BLOCK, BLOCK) for c in range(i)]
        row += [(place + i, i, 0, HALF, HALF), (place + i, i, HALF, HALF, BLOCK)]
        pieces.append(row)
    return pieces


def folded(values, combine):
    result = values[:, :LANES]
    for b in range(1, values.shape[1] // LANES):
        result = combine(result, values[:, b * LANES : (b + 1) * LANES])
    return result


def joined(source_ref, start):
    rows = source_ref.shape[2]
    blocks = [source_ref[start // rows + b] for b in range(HALF // rows)]
    return jnp.concatenate(blocks, axis=1)


def weight_kernel(query_ref, key_ref, out_ref, scores):
    total = query_ref.shape[0] * query_ref.shape[2]
    score_scale = 1.0 / math.sqrt(ATT_DIM)
    for start in range(0, total, HALF):
        block, offset = start // BLOCK, start % BLOCK
        queries = joined(query_ref, start).T
        spans = [slice(c, c + HALF) for c in range(0, start + HALF, HALF)]
        top = None
        for span in spans:
            values = (
                jnp.dot(queries, joined(key_ref, span.start), preferred_element_type=jnp.float32)
                * score_scale
            )
            if span.start == start:
                query_pos = lax.broadcasted_iota(jnp.int32, values.shape, 0)
                key_pos = lax.broadcasted_iota(jnp.int32, values.shape, 1)
                values = jnp.where(key_pos <= query_pos, values, -jnp.inf)
            scores[:, span] = values
            part = folded(values, jnp.maximum)
            top = part if top is None else jnp.maximum(top, part)
        top = jnp.max(top, axis=1, keepdims=True)
        norm = 0.0
        for span in spans:
            values = jnp.exp(scores[:, span] - top)
            scores[:, span] = values
            norm = norm + folded(values, jnp.add)
        inverse = 1.0 / jnp.sum(norm, axis=1, keepdims=True)
        for span in spans:
            values = (scores[:, span] * inverse).astype(jnp.bfloat16)
            other, column = span.start // BLOCK, span.start % BLOCK
            place = block * (block + 1) // 2 + other
            out_ref[place, offset : offset + HALF, column : column + HALF] = values


def attention_weights(queries, keys):
    sources, _, rows = keys.shape
    blocks = len(weight_blocks(sources * rows))
    vmem = pl.BlockSpec(memory_space=pltpu.VMEM)
    return pl.pallas_call(
        weight_kernel,
        in_specs=[vmem] * 2,
        out_specs=vmem,
        out_shape=jax.ShapeDtypeStruct((blocks, BLOCK, BLOCK), jnp.bfloat16),
        scratch_shapes=[pltpu.VMEM((HALF, sources * rows), jnp.float32)],
        compiler_params=PARAMS,
    )(queries, keys)


def mix_kernel(value_ref, weight_ref, out_ref, values, sems, *buffers):
    rows = value_ref.shape[2]
    total = value_ref.shape[0] * rows
    per_block = BLOCK // rows
    pieces = weight_pieces(total)
    copies = []
    for row in pieces:
        copies.append([])
        for place, _, start, count, span in row:
            n = sum(len(done) for done in copies)
            source = weight_ref.at[place, start : start + count, :span]
            copies[-1].append((pltpu.make_async_copy(source, buffers[n], sems.at[n]), buffers[n]))
    for row in copies[:2]:
        for copy, _ in row:
            copy.start()
    padding = jnp.zeros((PADDED - ATT_DIM, rows), jnp.bfloat16)
    for b in range(value_ref.shape[0]):
        padded = jnp.concatenate([value_ref[b], padding], axis=0)
        values[b * rows : (b + 1) * rows] = padded.T
    for i, row in enumerate(copies):
        for copy, _ in row:
            copy.wait()
        if i + 2 < len(copies):
            for copy, _ in copies[i + 2]:
                copy.start()
        for first in range(0, BLOCK, STRIP):
            result = 0.0
            for (_, c, start, count, span), (_, buffer) in zip(pieces[i], row):
                if not start <= first < start + count:
                    continue
                part = values[c * BLOCK : c * BLOCK + span]
                weights = buffer[first - start : first - start + STRIP]
                result = jnp.dot(weights, part, preferred_element_type=jnp.float32) + result
            result = result.astype(jnp.bfloat16)
            for b in range(STRIP // rows):
                turned = result[b * rows : (b + 1) * rows].T
                out_ref[i * per_block + first // rows + b] = turned[:ATT_DIM]


def mixed(weights, values):
    sources, _, rows = values.shape
    pieces = [piece for row in weight_pieces(sources * rows) for piece in row]
    vmem = pl.BlockSpec(memory_space=pltpu.VMEM)
    return pl.pallas_call(
        mix_kernel,
        in_specs=[vmem, pl.BlockSpec(memory_space=pltpu.HBM)],
        out_specs=vmem,
        out_shape=jax.ShapeDtypeStruct((sources, ATT_DIM, rows), jnp.bfloat16),
        scratch_shapes=[
            pltpu.VMEM((sources * rows, PADDED), jnp.bfloat16),
            pltpu.SemaphoreType.DMA((len(pieces),)),
        ]
        + [pltpu.VMEM((count, span), jnp.bfloat16) for _, _, _, count, span in pieces],
        compiler_params=PARAMS,
    )(values, weights)


def local(
    conv_input,
    gate_input,
    step_raw,
    step_bias,
    decay_log,
    skip_weight,
    conv_weight,
    conv_bias,
    norm_gain,
    queries,
    key_rows,
):
    row_count = conv_input.shape[0]
    share = HEADS // GROUPS
    before = shifted(conv_input[row_count - (CONV - 1) :], "ctx", 1)
    head_queries = exchanged(turned_rows(queries))

    padded = jnp.concatenate([before.astype(jnp.float32), conv_input.astype(jnp.float32)], axis=0)
    inputs = convolve(padded, conv_weight, conv_bias, row_count)
    step_rates = jnp.minimum(jax.nn.softplus(step_raw + step_bias[None, :]), dt_cap)
    decay_rate = -jnp.exp(decay_log)
    running = jnp.cumsum(step_rates * decay_rate[None], axis=0)
    values = inputs[:, :INNER].astype(jnp.float32)
    writes = inputs[:, INNER : INNER + GROUPS * STATE].reshape(row_count, GROUPS, STATE)
    readout_low = inputs[:, INNER + GROUPS * STATE :]
    readout = readout_low.reshape(row_count, GROUPS, STATE)
    carry_weight = jnp.exp(running[-1][None] - running) * step_rates
    near = lax.rem(lax.axis_index("ctx"), NEAR)
    parts = block_states(
        near[None],
        inputs,
        inputs[:, INNER : INNER + GROUPS * STATE],
        carry_weight,
        jnp.exp(running[-1]),
    )
    running_heads = running.T.reshape(GROUPS, share, row_count)
    rates_heads = step_rates.T.reshape(GROUPS, share, row_count)
    positions = jnp.arange(row_count, dtype=jnp.int32)
    causal = (positions[:, None] >= positions[None, :])[None, None]
    spread = running_heads[:, :, :, None] - running_heads[:, :, None, :]
    fading = jnp.exp(jnp.where(causal, spread, -jnp.inf))
    intersection = jnp.einsum("tgn,sgn->gts", readout, writes, preferred_element_type=jnp.float32)
    mixing = intersection[:, None] * fading * rates_heads[:, :, None, :]
    grouped = values.reshape(row_count, GROUPS, share, HEAD_DIM)
    inside = jnp.einsum("gkts,sgkp->tgkp", mixing, grouped, precision=HIGHEST)

    parts = [parts[0]] + [near_shifted(parts[r], r) for r in range(1, NEAR)]
    inside, *parts = lax.optimization_barrier((inside, *parts))
    total = group_state(near[None], parts)
    head_queries, total = lax.optimization_barrier((head_queries, total))
    far = lax.axis_index("ctx") // NEAR
    group_in = far_exchanged(scanned(far[None], far_exchanged(total)))
    turned_keys, group_in = lax.optimization_barrier((turned_rows(key_rows), group_in))
    head_keys = exchanged(turned_keys)
    entering = entering_states(near[None], parts, group_in)
    states = [entering[0]] + [near_shifted(entering[r], r) for r in range(1, NEAR)]
    order = lax.rem(near + NEAR - jnp.arange(NEAR), NEAR)
    readout_parts = readout_low.reshape(row_count, GROUPS, ROW_PARTS, PART_ROWS)
    readout_parts = jnp.take(readout_parts, order, axis=2).reshape(row_count, GROUPS, STATE)
    readout_parts = readout_parts.transpose(1, 0, 2)

    gate = jax.nn.silu(gate_input.astype(jnp.float32))
    base = (inside.reshape(row_count, INNER) + per_channel(skip_weight)[None] * values) * gate
    factor = per_channel(jnp.exp(running)) * gate

    mamba_out, turned_out = normed_output(readout_parts, states, base, factor, norm_gain)
    weights = attention_weights(head_queries, head_keys)
    attended_heads = mixed(weights, exchanged(turned_out))
    attended = exchanged(attended_heads)
    attended = attended.transpose(2, 0, 1).reshape(row_count, INNER)
    return (mamba_out, attended)


def solution(mesh):
    rows = P(("dp", "ctx"), None)
    placed = (rows, rows, rows, P(), P(), P(), P(), P(), P(), rows, rows)
    return jax.shard_map(
        local, mesh=mesh, in_specs=placed, out_specs=(rows, rows), check_vma=False
    )
```

```python
import functools
import math

import jax
import jax.numpy as jnp
from jax import lax
from jax.experimental import pallas as pl
from jax.experimental.pallas import tpu as pltpu
from jax.sharding import PartitionSpec as P

HEADS = 112
HEAD_DIM = 64
STATE = 64
GROUPS = 2
CONV = 4
ATT_DIM = 224
INNER = HEADS * HEAD_DIM
SHARE = INNER // GROUPS

ROW_PARTS = 4
COL_PARTS = 8
PART_ROWS = STATE // ROW_PARTS
PART_COLS = INNER // COL_PARTS
LANES = 128
PART_TILES = PART_COLS // LANES
PART_HEADS = PART_COLS // HEAD_DIM
STATE_ROWS = PART_TILES * PART_ROWS

BLOCK = 1024
HALF = BLOCK // 2
STRIP = 256
PADDED = 256
NEAR = ROW_PARTS

dt_cap = 3.0
eps = 1e-05
HIGHEST = lax.Precision.HIGHEST
VMEM_LIMIT = 48 * 1024 * 1024
PARAMS = pltpu.CompilerParams(vmem_limit_bytes=VMEM_LIMIT)


def far_size():
    return lax.axis_size("ctx") // NEAR


def shifted(array, axis, by):
    size = lax.axis_size(axis)
    pairs = [(i, i + by) for i in range(size) if 0 <= i + by < size]
    return lax.ppermute(array, axis, pairs)


def near_shifted(array, by):
    pairs = [
        (far * NEAR + near, far * NEAR + (near + by) % NEAR)
        for far in range(far_size())
        for near in range(NEAR)
    ]
    return lax.ppermute(array, "ctx", pairs)


def exchanged(array):
    return lax.all_to_all(array, "ctx", 0, 0, tiled=True)


def far_exchanged(array):
    groups = [[far * NEAR + near for far in range(far_size())] for near in range(NEAR)]
    return lax.all_to_all(array, "ctx", 0, 0, axis_index_groups=groups, tiled=True)


def convolve(padded, conv_weight, conv_bias, row_count):
    total = conv_bias[None, :] + conv_weight[0][None, :] * padded[0:row_count]
    for tap_index in range(1, conv_weight.shape[0]):
        total = total + conv_weight[tap_index][None, :] * padded[tap_index : tap_index + row_count]
    return jax.nn.silu(total).astype(jnp.bfloat16)


def head_columns(first, count):
    head = lax.broadcasted_iota(jnp.int32, (LANES, count), 0)
    channel = lax.broadcasted_iota(jnp.int32, (LANES, count), 1) + first
    return (channel // HEAD_DIM == head).astype(jnp.float32).astype(jnp.bfloat16)


def pieces_of(value):
    high = value.astype(jnp.bfloat16)
    rest = value - high.astype(jnp.float32)
    middle = rest.astype(jnp.bfloat16)
    low = (rest - middle.astype(jnp.float32)).astype(jnp.bfloat16)
    return high, middle, low


def per_channel(by_head):
    heads = jnp.arange(HEADS)[:, None]
    channels = jnp.arange(INNER)[None, :] // HEAD_DIM
    return jnp.dot(by_head, (heads == channels).astype(jnp.float32), precision=HIGHEST)


def turn_kernel(source_ref, out_ref):
    turned = source_ref[...].T
    for h in range(out_ref.shape[0]):
        out_ref[h] = turned[h * ATT_DIM : (h + 1) * ATT_DIM]


def turned_rows(source):
    rows, width = source.shape
    heads = width // ATT_DIM
    steps = 2
    return pl.pallas_call(
        turn_kernel,
        grid=(steps,),
        in_specs=[pl.BlockSpec((rows, width // steps), lambda i: (0, i))],
        out_specs=pl.BlockSpec((heads // steps, ATT_DIM, rows), lambda i: (i, 0, 0)),
        out_shape=jax.ShapeDtypeStruct((heads, ATT_DIM, rows), source.dtype),
        compiler_params=PARAMS,
    )(source)


PART_LINES = STATE_ROWS + PART_ROWS


def rounded_rows(values):
    rows = [piece.astype(jnp.float32) for piece in pieces_of(values)]
    rows.append(jnp.zeros((PART_ROWS - 3, LANES), jnp.float32))
    return jnp.concatenate(rows, axis=0).astype(jnp.bfloat16)


def state_kernel(near_ref, input_ref, write_ref, carry_ref, decay_ref, out_ref, state):
    step = pl.program_id(0)
    per_step = out_ref.shape[1]
    decays = rounded_rows(decay_ref[...])
    carry = pieces_of(carry_ref[...])
    for c in range(per_step):
        columns = head_columns((step * per_step + c) * PART_COLS, PART_COLS)
        spread = sum(jnp.dot(p, columns, preferred_element_type=jnp.float32) for p in carry)
        source = input_ref[:, c * PART_COLS : (c + 1) * PART_COLS].astype(jnp.float32)
        weighted = source * spread
        high = weighted.astype(jnp.bfloat16)
        low = (weighted - high.astype(jnp.float32)).astype(jnp.bfloat16)
        state[...] = jnp.dot(write_ref[...], high, preferred_element_type=jnp.float32) + jnp.dot(
            write_ref[...], low, preferred_element_type=jnp.float32
        )
        for r in range(NEAR):
            part = lax.rem(near_ref[0] + r, NEAR)
            rows = state[pl.ds(pl.multiple_of(part * PART_ROWS, PART_ROWS), PART_ROWS)]
            rows = rows.astype(jnp.bfloat16)
            for tile in range(PART_TILES):
                out_ref[r, c, tile * PART_ROWS : (tile + 1) * PART_ROWS] = rows[
                    :, tile * LANES : (tile + 1) * LANES
                ]
            out_ref[r, c, STATE_ROWS:] = decays


def block_states(near, inputs, writes, carry, decay):
    rows = inputs.shape[0]
    steps = 4
    per_step = COL_PARTS // steps
    padding = ((0, 0), (0, LANES - HEADS))
    whole = pl.BlockSpec(memory_space=pltpu.SMEM)
    return pl.pallas_call(
        state_kernel,
        grid=(steps,),
        in_specs=[
            whole,
            pl.BlockSpec((rows, per_step * PART_COLS), lambda i: (0, i)),
            pl.BlockSpec((STATE, rows), lambda i: (i // (steps // GROUPS), 0)),
            pl.BlockSpec((rows, LANES), lambda i: (0, 0)),
            pl.BlockSpec((1, LANES), lambda i: (0, 0)),
        ],
        out_specs=pl.BlockSpec((NEAR, per_step, PART_LINES, LANES), lambda i: (0, i, 0, 0)),
        out_shape=jax.ShapeDtypeStruct((NEAR, COL_PARTS, PART_LINES, LANES), jnp.bfloat16),
        scratch_shapes=[pltpu.VMEM((STATE, PART_COLS), jnp.float32)],
        compiler_params=PARAMS,
    )(near, inputs, writes.T, jnp.pad(carry, padding), jnp.pad(decay[None], padding))


def decay_row(part):
    lines = part[STATE_ROWS : STATE_ROWS + 8].astype(jnp.float32)
    return jnp.sum(lines, axis=0, keepdims=True)


def spread_decay(part, columns):
    spread = jnp.dot(part[STATE_ROWS:], columns, preferred_element_type=jnp.float32)
    return jnp.sum(spread[:8], axis=0, keepdims=True)


def advanced(state, part, columns):
    decay = spread_decay(part, columns)
    return [
        state[t] * decay[:, t * LANES : (t + 1) * LANES]
        + part[t * PART_ROWS : (t + 1) * PART_ROWS].astype(jnp.float32)
        for t in range(PART_TILES)
    ]


def no_state():
    return [jnp.zeros((PART_ROWS, LANES), jnp.float32) for _ in range(PART_TILES)]


def in_order(near_ref, refs, ordered):
    for r in range(NEAR):
        ordered[lax.rem(near_ref[0] + NEAR - r, NEAR)] = refs[r][...]


def group_kernel(near_ref, *refs):
    out_ref, ordered = refs[NEAR:]
    in_order(near_ref, refs[:NEAR], ordered)
    decay = decay_row(ordered[0, 0])
    for near in range(1, NEAR):
        decay = decay * decay_row(ordered[near, 0])
    decays = rounded_rows(decay)

    def combine(c, carry):
        columns = head_columns(c * PART_COLS, PART_COLS)
        state = no_state()
        for near in range(NEAR):
            state = advanced(state, ordered[near, c], columns)
        for t in range(PART_TILES):
            out_ref[c, t * PART_ROWS : (t + 1) * PART_ROWS] = state[t].astype(jnp.bfloat16)
        out_ref[c, STATE_ROWS:] = decays
        return carry

    lax.fori_loop(0, COL_PARTS, combine, 0)


def group_state(near, parts):
    vmem = pl.BlockSpec(memory_space=pltpu.VMEM)
    return pl.pallas_call(
        group_kernel,
        in_specs=[pl.BlockSpec(memory_space=pltpu.SMEM)] + [vmem] * NEAR,
        out_specs=vmem,
        out_shape=jax.ShapeDtypeStruct(parts[0].shape, jnp.bfloat16),
        scratch_shapes=[pltpu.VMEM((NEAR,) + parts[0].shape, jnp.bfloat16)],
        compiler_params=PARAMS,
    )(near, *parts)


def scan_kernel(far_ref, recv_ref, out_ref):
    columns = head_columns(far_ref[0] * PART_COLS, PART_COLS)
    groups = recv_ref.shape[0]
    state = no_state()
    for group in range(groups):
        for t in range(PART_TILES):
            rows = slice(t * PART_ROWS, (t + 1) * PART_ROWS)
            out_ref[group, rows] = state[t].astype(jnp.bfloat16)
        if group < groups - 1:
            state = advanced(state, recv_ref[group], columns)


def scanned(far, received):
    vmem = pl.BlockSpec(memory_space=pltpu.VMEM)
    return pl.pallas_call(
        scan_kernel,
        in_specs=[pl.BlockSpec(memory_space=pltpu.SMEM), vmem],
        out_specs=vmem,
        out_shape=jax.ShapeDtypeStruct((received.shape[0], STATE_ROWS, LANES), jnp.bfloat16),
        compiler_params=PARAMS,
    )(far, received)


def enter_kernel(near_ref, *refs):
    group_ref, out_ref, ordered = refs[NEAR:]
    in_order(near_ref, refs[:NEAR], ordered)

    def enter(c, carry):
        columns = head_columns(c * PART_COLS, PART_COLS)
        state = [
            group_ref[c, t * PART_ROWS : (t + 1) * PART_ROWS].astype(jnp.float32)
            for t in range(PART_TILES)
        ]
        for near in range(NEAR):
            place = lax.rem(near - near_ref[0] + NEAR, NEAR)
            for t in range(PART_TILES):
                out_ref[place, c, t * PART_ROWS : (t + 1) * PART_ROWS] = state[t].astype(
                    jnp.bfloat16
                )
            if near < NEAR - 1:
                state = advanced(state, ordered[near, c], columns)
        return carry

    lax.fori_loop(0, COL_PARTS, enter, 0)


def entering_states(near, parts, group_in):
    vmem = pl.BlockSpec(memory_space=pltpu.VMEM)
    return pl.pallas_call(
        enter_kernel,
        in_specs=[pl.BlockSpec(memory_space=pltpu.SMEM)] + [vmem] * (NEAR + 1),
        out_specs=vmem,
        out_shape=jax.ShapeDtypeStruct((NEAR, COL_PARTS, STATE_ROWS, LANES), jnp.bfloat16),
        scratch_shapes=[pltpu.VMEM((NEAR,) + parts[0].shape, jnp.bfloat16)],
        compiler_params=PARAMS,
    )(near, *parts, group_in)


def norm_kernel(readout_ref, *refs):
    states = refs[:NEAR]
    base_ref, factor_ref, gain_ref, out_ref, turned_ref = refs[NEAR:]
    readout = readout_ref[0]
    held = []
    total = 0.0
    chunks = out_ref.shape[1] // PART_COLS
    for c in range(chunks):
        columns = slice(c * PART_COLS, (c + 1) * PART_COLS)
        tiles = []
        for tile in range(PART_TILES):
            rows = slice(tile * PART_ROWS, (tile + 1) * PART_ROWS)
            tiles.append(jnp.concatenate([state[c, rows] for state in states], axis=0))
        state = jnp.concatenate(tiles, axis=1)
        across = jnp.dot(readout, state, preferred_element_type=jnp.float32)
        values = base_ref[:, columns] + across * factor_ref[:, columns]
        held.append(values)
        total = total + jnp.sum(values * values, axis=1, keepdims=True)
    scale = lax.rsqrt(total / SHARE + eps)
    per_chunk = PART_COLS // ATT_DIM
    for c in range(chunks):
        columns = slice(c * PART_COLS, (c + 1) * PART_COLS)
        normed = (held[c] * scale * gain_ref[:, columns]).astype(jnp.bfloat16)
        out_ref[:, columns] = normed
        turned = normed.T
        for h in range(per_chunk):
            turned_ref[c * per_chunk + h] = turned[h * ATT_DIM : (h + 1) * ATT_DIM]


def normed_output(readout, states, base, factor, norm_gain):
    rows = base.shape[0]
    chunks = COL_PARTS // GROUPS
    wide = pl.BlockSpec((rows, SHARE), lambda g: (0, g))
    heads = INNER // ATT_DIM // GROUPS
    part = pl.BlockSpec((chunks, STATE_ROWS, LANES), lambda g: (g, 0, 0))
    return pl.pallas_call(
        norm_kernel,
        grid=(GROUPS,),
        in_specs=[pl.BlockSpec((1, rows, STATE), lambda g: (g, 0, 0))]
        + [part] * NEAR
        + [wide, wide, pl.BlockSpec((1, SHARE), lambda g: (0, g))],
        out_specs=[wide, pl.BlockSpec((heads, ATT_DIM, rows), lambda g: (g, 0, 0))],
        out_shape=[
            jax.ShapeDtypeStruct((rows, INNER), jnp.bfloat16),
            jax.ShapeDtypeStruct((GROUPS * heads, ATT_DIM, rows), jnp.bfloat16),
        ],
        compiler_params=PARAMS,
    )(readout, *states, base, factor, norm_gain.reshape(1, INNER))


def weight_pieces(total):
    pieces = []
    for i in range(total // BLOCK):
        row = [(c, 0, BLOCK, BLOCK) for c in range(i)]
        pieces.append(row + [(i, 0, HALF, HALF), (i, HALF, HALF, BLOCK)])
    return pieces


def weight_kernel(query_ref, key_ref, out_ref, scores):
    step = pl.program_id(0)
    rows = key_ref.shape[2]
    per_block = BLOCK // rows
    queries = jnp.concatenate([query_ref[b] for b in range(per_block)], axis=1).T
    score_scale = 1.0 / math.sqrt(ATT_DIM)

    def raw(chunk):
        keys = [key_ref[chunk * per_block + b] for b in range(per_block)]
        keys = jnp.concatenate(keys, axis=1)
        return jnp.dot(queries, keys, preferred_element_type=jnp.float32) * score_scale

    def folded(values, combine):
        result = values[:, :LANES]
        for b in range(1, BLOCK // LANES):
            result = combine(result, values[:, b * LANES : (b + 1) * LANES])
        return result

    def first(chunk, top):
        values = raw(chunk)
        scores[chunk] = values
        return jnp.maximum(top, folded(values, jnp.maximum))

    top = lax.fori_loop(0, step, first, jnp.full((BLOCK, LANES), -jnp.inf, jnp.float32))
    query_pos = lax.broadcasted_iota(jnp.int32, (BLOCK, BLOCK), 0)
    key_pos = lax.broadcasted_iota(jnp.int32, (BLOCK, BLOCK), 1)
    values = jnp.where(key_pos <= query_pos, raw(step), -jnp.inf)
    scores[step] = values
    top = jnp.maximum(top, folded(values, jnp.maximum))
    top = jnp.max(top, axis=1, keepdims=True)

    def second(chunk, total):
        values = jnp.exp(scores[chunk] - top)
        scores[chunk] = values
        return total + folded(values, jnp.add)

    total = lax.fori_loop(0, step + 1, second, jnp.zeros((BLOCK, LANES), jnp.float32))
    inverse = 1.0 / jnp.sum(total, axis=1, keepdims=True)

    def third(chunk, carry):
        out_ref[0, chunk] = (scores[chunk] * inverse).astype(jnp.bfloat16)
        return carry

    lax.fori_loop(0, step + 1, third, 0)


def attention_weights(queries, keys):
    sources, _, rows = keys.shape
    steps = sources * rows // BLOCK
    return pl.pallas_call(
        weight_kernel,
        grid=(steps,),
        in_specs=[
            pl.BlockSpec((BLOCK // rows, ATT_DIM, rows), lambda i: (i, 0, 0)),
            pl.BlockSpec((sources, ATT_DIM, rows), lambda i: (0, 0, 0)),
        ],
        out_specs=pl.BlockSpec((1, steps, BLOCK, BLOCK), lambda i: (i, 0, 0, 0)),
        out_shape=jax.ShapeDtypeStruct((steps, steps, BLOCK, BLOCK), jnp.bfloat16),
        scratch_shapes=[pltpu.VMEM((steps, BLOCK, BLOCK), jnp.float32)],
        compiler_params=PARAMS,
    )(queries, keys)


def mix_kernel(value_ref, weight_ref, out_ref, values, sems, *buffers):
    rows = value_ref.shape[2]
    total = value_ref.shape[0] * rows
    per_block = BLOCK // rows
    pieces = weight_pieces(total)
    copies = []
    for i, row in enumerate(pieces):
        copies.append([])
        for c, start, count, span in row:
            n = sum(len(done) for done in copies)
            source = weight_ref.at[i, c, start : start + count, :span]
            copies[-1].append((pltpu.make_async_copy(source, buffers[n], sems.at[n]), buffers[n]))
    for row in copies[:2]:
        for copy, _ in row:
            copy.start()
    padding = jnp.zeros((PADDED - ATT_DIM, rows), jnp.bfloat16)
    for b in range(value_ref.shape[0]):
        padded = jnp.concatenate([value_ref[b], padding], axis=0)
        values[b * rows : (b + 1) * rows] = padded.T
    for i, row in enumerate(copies):
        for copy, _ in row:
            copy.wait()
        if i + 2 < len(copies):
            for copy, _ in copies[i + 2]:
                copy.start()
        for first in range(0, BLOCK, STRIP):
            result = 0.0
            for (c, start, count, span), (_, buffer) in zip(pieces[i], row):
                if not start <= first < start + count:
                    continue
                part = values[c * BLOCK : c * BLOCK + span]
                weights = buffer[first - start : first - start + STRIP]
                result = jnp.dot(weights, part, preferred_element_type=jnp.float32) + result
            result = result.astype(jnp.bfloat16)
            for b in range(STRIP // rows):
                turned = result[b * rows : (b + 1) * rows].T
                out_ref[i * per_block + first // rows + b] = turned[:ATT_DIM]


def mixed(weights, values):
    sources, _, rows = values.shape
    pieces = [piece for row in weight_pieces(sources * rows) for piece in row]
    vmem = pl.BlockSpec(memory_space=pltpu.VMEM)
    return pl.pallas_call(
        mix_kernel,
        in_specs=[vmem, pl.BlockSpec(memory_space=pltpu.HBM)],
        out_specs=vmem,
        out_shape=jax.ShapeDtypeStruct((sources, ATT_DIM, rows), jnp.bfloat16),
        scratch_shapes=[
            pltpu.VMEM((sources * rows, PADDED), jnp.bfloat16),
            pltpu.SemaphoreType.DMA((len(pieces),)),
        ]
        + [pltpu.VMEM((count, span), jnp.bfloat16) for _, _, count, span in pieces],
        compiler_params=PARAMS,
    )(values, weights)


def local(
    conv_input,
    gate_input,
    step_raw,
    step_bias,
    decay_log,
    skip_weight,
    conv_weight,
    conv_bias,
    norm_gain,
    queries,
    key_rows,
):
    row_count = conv_input.shape[0]
    share = HEADS // GROUPS
    before = shifted(conv_input[row_count - (CONV - 1) :], "ctx", 1)
    head_queries = exchanged(turned_rows(queries))

    padded = jnp.concatenate([before.astype(jnp.float32), conv_input.astype(jnp.float32)], axis=0)
    inputs = convolve(padded, conv_weight, conv_bias, row_count)
    step_rates = jnp.minimum(jax.nn.softplus(step_raw + step_bias[None, :]), dt_cap)
    decay_rate = -jnp.exp(decay_log)
    running = jnp.cumsum(step_rates * decay_rate[None], axis=0)
    values = inputs[:, :INNER].astype(jnp.float32)
    writes = inputs[:, INNER : INNER + GROUPS * STATE].reshape(row_count, GROUPS, STATE)
    readout_low = inputs[:, INNER + GROUPS * STATE :]
    readout = readout_low.reshape(row_count, GROUPS, STATE)
    carry_weight = jnp.exp(running[-1][None] - running) * step_rates
    near = lax.rem(lax.axis_index("ctx"), NEAR)
    parts = block_states(
        near[None],
        inputs,
        inputs[:, INNER : INNER + GROUPS * STATE],
        carry_weight,
        jnp.exp(running[-1]),
    )
    running_heads = running.T.reshape(GROUPS, share, row_count)
    rates_heads = step_rates.T.reshape(GROUPS, share, row_count)
    positions = jnp.arange(row_count, dtype=jnp.int32)
    causal = (positions[:, None] >= positions[None, :])[None, None]
    spread = running_heads[:, :, :, None] - running_heads[:, :, None, :]
    fading = jnp.exp(jnp.where(causal, spread, -jnp.inf))
    intersection = jnp.einsum("tgn,sgn->gts", readout, writes, preferred_element_type=jnp.float32)
    mixing = intersection[:, None] * fading * rates_heads[:, :, None, :]
    grouped = values.reshape(row_count, GROUPS, share, HEAD_DIM)
    inside = jnp.einsum("gkts,sgkp->tgkp", mixing, grouped, precision=HIGHEST)

    parts = [parts[0]] + [near_shifted(parts[r], r) for r in range(1, NEAR)]
    inside, *parts = lax.optimization_barrier((inside, *parts))
    total = group_state(near[None], parts)
    head_queries, total = lax.optimization_barrier((head_queries, total))
    far = lax.axis_index("ctx") // NEAR
    group_in = far_exchanged(scanned(far[None], far_exchanged(total)))
    turned_keys, group_in = lax.optimization_barrier((turned_rows(key_rows), group_in))
    head_keys = exchanged(turned_keys)
    entering = entering_states(near[None], parts, group_in)
    states = [entering[0]] + [near_shifted(entering[r], r) for r in range(1, NEAR)]
    order = lax.rem(near + NEAR - jnp.arange(NEAR), NEAR)
    readout_parts = readout_low.reshape(row_count, GROUPS, ROW_PARTS, PART_ROWS)
    readout_parts = jnp.take(readout_parts, order, axis=2).reshape(row_count, GROUPS, STATE)
    readout_parts = readout_parts.transpose(1, 0, 2)

    gate = jax.nn.silu(gate_input.astype(jnp.float32))
    base = (inside.reshape(row_count, INNER) + per_channel(skip_weight)[None] * values) * gate
    factor = per_channel(jnp.exp(running)) * gate

    mamba_out, turned_out = normed_output(readout_parts, states, base, factor, norm_gain)
    weights = attention_weights(head_queries, head_keys)
    attended_heads = mixed(weights, exchanged(turned_out))
    attended = exchanged(attended_heads)
    attended = attended.transpose(2, 0, 1).reshape(row_count, INNER)
    return (mamba_out, attended)


def solution(mesh):
    rows = P(("dp", "ctx"), None)
    placed = (rows, rows, rows, P(), P(), P(), P(), P(), P(), rows, rows)
    return jax.shard_map(
        local, mesh=mesh, in_specs=placed, out_specs=(rows, rows), check_vma=False
    )
```
